256 devices in a mesh: lon: 64 (over z, x, y_hi), lat: 4 (over y_lo, core).
Axes of the slice: x: 4, y: 4 (y_hi: 2, y_lo: 2; y = y_hi * 2 + y_lo), z: 8, core: 2. Of those that a mesh axis runs over, the one named last changes fastest.
Arguments:
- temp: float32 [10, 128, 8192], P(None, 'lat', 'lon'), may hold values from -6 to 6
- salt: float32 [10, 128, 8192], P(None, 'lat', 'lon'), may hold values from -6 to 6
- u_vel: float32 [10, 128, 8192], P(None, 'lat', 'lon'), may hold values from -3 to 3
- v_vel: float32 [10, 128, 8192], P(None, 'lat', 'lon'), may hold values from -3 to 3
- land_sea: int32 [10, 128, 8192], P(None, 'lat', 'lon'), may hold values 0 or 1
- partner: int32 [8192], P('lon'), may hold values from 0 to 8191, as said below
- kappa_h: float32 [10], replicated, may hold values from 0.02 to 0.25
- kappa_v: float32 [9], replicated, may hold values from 0.02 to 0.12
Outputs:
- temp_next: float32 [10, 128, 8192], P(None, 'lat', 'lon')
- salt_next: float32 [10, 128, 8192], P(None, 'lat', 'lon')
The draws below stay inside these ranges and needn't reach their ends.
Inputs may be any that keep to these rules, and one draw needn't show every extreme that they name: partner[i] = (s - i) mod 8192 for one s; every longitude appears once.
All inputs are finite; a program needn't handle non-finite values. No bound on the sum of `land_sea` on one device may be relied on, other than what follows from the above.
Results may differ from the reference program's by a relative error of at most 0.00005.
Values sent between devices are 32-bit elements; how exact they have to be, the bound alone decides.
A program may use at most 128 MiB of HBM per device.

```python
import jax
import jax.numpy as jnp

LEV = 10
STEPS = 2
NX = 8192
NY = 128


def draw_partner(key, part):
    key = jax.random.fold_in(key, 7)
    offset = jax.random.randint(key, (), 0, NX, dtype=jnp.int32)
    return ((offset - jnp.arange(NX, dtype=jnp.int32)) % NX).astype(jnp.int32)


def plant(entries, key, low, high):
    index_at = [jax.random.randint(jax.random.fold_in(key, axis), (), 0, length) for axis, length in enumerate(entries.shape)]
    longest = entries.shape.index(max(entries.shape))
    next_to = index_at[:longest] + [(index_at[longest] + 1) % entries.shape[longest]] + index_at[longest + 1:]
    return entries.at[tuple(index_at)].set(low).at[tuple(next_to)].set(high)


def block_levels(own_key, dims, split, smallest, top_value):
    loudness, own = 1.0, jax.random.fold_in(own_key, 6)
    for position, blocks in split:
        steps = jnp.exp(jax.random.uniform(jax.random.fold_in(own, position), (blocks,), jnp.float32, smallest / len(split), top_value / len(split)))
        loudness = loudness * jnp.repeat(steps, dims[position] // blocks).reshape([-1 if axis == position else 1 for axis in range(len(dims))])
    return loudness


def bell_draw(stream_key, extent, deviation, bound, pieces=(), kind=jnp.bfloat16):
    level = block_levels(stream_key, extent, pieces, -0.22, 0.18) if pieces else 1.0
    drawn = jax.random.normal(stream_key, extent, jnp.float32) * deviation * level
    return jnp.minimum(jnp.maximum(drawn, -bound), bound).astype(kind)


def setup_inputs(seed: int = 0) -> dict:
    key_of = jax.random.split(jax.random.key(seed), 9)
    temp = bell_draw(key_of[0], (LEV, NY, NX), 1.0, 6.0, ((1, 4), (2, 64)), jnp.float32)
    salt = bell_draw(key_of[1], (LEV, NY, NX), 1.0, 6.0, ((1, 4), (2, 64)), jnp.float32)
    u_vel = bell_draw(key_of[2], (LEV, NY, NX), 0.3, 3.0, ((1, 4), (2, 64)), jnp.float32)
    v_vel = bell_draw(key_of[3], (LEV, NY, NX), 0.3, 3.0, ((1, 4), (2, 64)), jnp.float32)
    land_sea = plant((jax.random.randint(key_of[4], (LEV, NY, NX), 0, 5) < 4).astype(jnp.int32), jax.random.fold_in(key_of[4], 1), 0, 1)
    partner = draw_partner(jax.random.fold_in(key_of[8], 71), 0)
    kappa_h = jnp.clip(jax.random.uniform(key_of[6], (LEV,), jnp.float32, 0.02, 0.25), 0.02, 0.25)
    kappa_v = jnp.clip(jax.random.uniform(key_of[7], (LEV - 1,), jnp.float32, 0.02, 0.12), 0.02, 0.12)
    return dict(temp=temp, salt=salt, u_vel=u_vel, v_vel=v_vel, land_sea=land_sea, partner=partner, kappa_h=kappa_h, kappa_v=kappa_v)


def extend(stack, signs, partner):
    lon_pad = jnp.concatenate([stack[..., -2:], stack, stack[..., :2]], axis=-1)
    rows = stack[:, :, -2:, :][:, :, ::-1, :]
    folded = jnp.take(rows, partner, axis=3) * signs[:, None, None, None]
    lat_pad = jnp.concatenate([jnp.zeros_like(rows), stack, folded], axis=2)
    return lon_pad, lat_pad


def advance(tracer, tr_x, tr_y, vel_x, vel_y, mask_x, mask_y, ocean, kappa_h, kappa_v):
    width = tracer.shape[-1]
    height = tracer.shape[-2]
    diffuse = kappa_h[:, None, None]
    west2, west1, east1, east2 = tr_x[..., 0:width + 1], tr_x[..., 1:width + 2], tr_x[..., 2:width + 3], tr_x[..., 3:width + 4]
    face_x = (7.0 * (west1 + east1) - (west2 + east2)) / 12.0
    speed_x = 0.5 * (vel_x[..., 1:width + 2] + vel_x[..., 2:width + 3])
    open_x = mask_x[..., 1:width + 2] * mask_x[..., 2:width + 3]
    flux_x = open_x * (speed_x * face_x - diffuse * (east1 - west1))
    south2, south1, north1, north2 = tr_y[..., 0:height + 1, :], tr_y[..., 1:height + 2, :], tr_y[..., 2:height + 3, :], tr_y[..., 3:height + 4, :]
    face_y = (7.0 * (south1 + north1) - (south2 + north2)) / 12.0
    speed_y = 0.5 * (vel_y[..., 1:height + 2, :] + vel_y[..., 2:height + 3, :])
    open_y = mask_y[..., 1:height + 2, :] * mask_y[..., 2:height + 3, :]
    flux_y = open_y * (speed_y * face_y - diffuse * (north1 - south1))
    open_z = ocean[1:] * ocean[:-1]
    flux_z = kappa_v[:, None, None] * open_z * (tracer[:, 1:] - tracer[:, :-1])
    edge = jnp.zeros_like(flux_z[:, :1])
    flux_z = jnp.concatenate([edge, flux_z, edge], axis=1)
    tendency = -(flux_x[..., 1:] - flux_x[..., :-1]) - (flux_y[..., 1:, :] - flux_y[..., :-1, :]) + flux_z[:, 1:] - flux_z[:, :-1]
    return tracer + ocean * tendency


def reference(temp, salt, u_vel, v_vel, land_sea, partner, kappa_h, kappa_v):
    ocean = land_sea.astype(jnp.float32)
    static = jnp.stack([u_vel, v_vel, ocean])
    static_x, static_y = extend(static, jnp.array([-1.0, -1.0, 1.0], jnp.float32), partner)
    tracer = jnp.stack([temp, salt])
    for step in range(STEPS):
        tr_x, tr_y = extend(tracer, jnp.array([1.0, 1.0], jnp.float32), partner)
        tracer = advance(tracer, tr_x, tr_y, static_x[0], static_y[1], static_x[2], static_y[2], ocean, kappa_h, kappa_v)
    return tracer[0], tracer[1]
```

```python
import functools

import jax
import jax.numpy as jnp
from jax import lax
from jax.experimental import pallas as pl
from jax.experimental.pallas import tpu as pltpu
from jax.sharding import PartitionSpec as P

STEPS = 2
GROUP = 4
LANES = 128
SLOT = 12
F32 = jnp.float32
MESH = pl.DeviceIdType.MESH
VMEM = pl.BlockSpec(memory_space=pltpu.VMEM)
SMEM = pl.BlockSpec(memory_space=pltpu.SMEM)


def roll(x, shift, axis=1):
    return pltpu.roll(x, shift, axis)


def pack(temp, salt, u_vel, v_vel, land, cols, north, south):
    levels, height, _ = temp.shape
    lane = lax.broadcasted_iota(jnp.int32, (height, LANES), 1)

    def level(l, held):
        base = l * SLOT
        t, s, v = temp[l], salt[l], v_vel[l]
        o = land[l].astype(F32)
        here = lane - base
        held = jnp.where((here >= 0) & (here < 4), roll(t, base + 2), held)
        held = jnp.where((here >= 4) & (here < 8), roll(s, base + 6), held)
        held = jnp.where((here >= 8) & (here < 10), roll(u_vel[l], base + 9), held)
        held = jnp.where((here >= 10) & (here < 12), roll(o, base + 11), held)
        for ref, lo, edge in ((north, height - 2, height - 1), (south, 0, 0)):
            ref[pl.ds(l, 1)] = t[lo : lo + 1]
            ref[pl.ds(levels + l, 1)] = t[lo + 1 : lo + 2]
            ref[pl.ds(2 * levels + l, 1)] = s[lo : lo + 1]
            ref[pl.ds(3 * levels + l, 1)] = s[lo + 1 : lo + 2]
            ref[pl.ds(4 * levels + l, 1)] = v[edge : edge + 1]
            ref[pl.ds(5 * levels + l, 1)] = o[edge : edge + 1]
        return held

    cols[...] = lax.fori_loop(0, levels, level, jnp.zeros((height, LANES), F32))


def pack_kernel(temp, salt, u_vel, v_vel, land, cols, north, south):
    pack(temp, salt, u_vel, v_vel, land, cols, north, south)


def exchange_kernel(branch, nlon, nlat, cols, north, south, west, east, below, above, send, recv):
    lon, lat = lax.axis_index("lon"), lax.axis_index("lat")
    top = lat == nlat - 1
    right, left = lax.rem(lon + 1, nlon), lax.rem(lon + nlon - 1, nlon)
    folds = [lax.rem(branch * GROUP - 1 + o - lon + 2 * nlon, nlon) for o in range(GROUP + 1)]
    barrier = pltpu.get_barrier_semaphore()

    def greet(a, b):
        pl.semaphore_signal(barrier, inc=1, device_id=(a, b), device_id_type=MESH)

    def copy(src, dst, slot, a, b):
        return pltpu.make_async_remote_copy(
            src_ref=src, dst_ref=dst, send_sem=send.at[slot], recv_sem=recv.at[slot], device_id=(a, b), device_id_type=MESH
        )

    def stay(o):
        return pltpu.make_async_copy(north, above.at[o], recv.at[3 + o])

    greet(right, lat)
    greet(left, lat)
    count = 2

    @pl.when(lat > 0)
    def _():
        greet(lon, lat - 1)

    @pl.when(lat < nlat - 1)
    def _():
        greet(lon, lat + 1)

    for f in folds:

        @pl.when(top & (f != lon))
        def _():
            greet(f, lat)

        count += (top & (f != lon)).astype(jnp.int32)
    count += (lat > 0).astype(jnp.int32) + (lat < nlat - 1).astype(jnp.int32)
    pl.semaphore_wait(barrier, count)

    for o, f in enumerate(folds):

        @pl.when(top & (f != lon))
        def _():
            copy(north, above.at[o], 3 + o, f, lat).start()

        @pl.when(top & (f == lon))
        def _():
            stay(o).start()

    to_right = copy(cols, west, 0, right, lat)
    to_left = copy(cols, east, 1, left, lat)
    to_right.start()
    to_left.start()
    to_north = copy(north, below, 2, lon, lax.rem(lat + 1, nlat))
    to_south = copy(south, above.at[0], 3, lon, lax.rem(lat + nlat - 1, nlat))

    @pl.when(lat < nlat - 1)
    def _():
        to_north.start()

    @pl.when(lat > 0)
    def _():
        copy_south(south, above, send, recv, lon, lat, nlat).start()

    to_right.wait()
    to_left.wait()

    @pl.when(lat > 0)
    def _():
        to_north.wait_recv()
        copy_south(south, above, send, recv, lon, lat, nlat).wait_send()

    @pl.when(lat < nlat - 1)
    def _():
        to_north.wait_send()
        to_south.wait_recv()

    for o, f in enumerate(folds):

        @pl.when(top & (f != lon))
        def _():
            copy(north, above.at[o], 3 + o, f, lat).wait()

        @pl.when(top & (f == lon))
        def _():
            stay(o).wait()


def copy_south(south, above, send, recv, lon, lat, nlat):
    return pltpu.make_async_remote_copy(
        src_ref=south,
        dst_ref=above.at[0],
        send_sem=send.at[4 + GROUP],
        recv_sem=recv.at[3],
        device_id=(lon, lax.rem(lat + nlat - 1, nlat)),
        device_id_type=MESH,
    )


def exchange(branch, nlon, nlat):
    def call(cols, north, south):
        rows = jax.ShapeDtypeStruct(north.shape, F32)
        side = jax.ShapeDtypeStruct(cols.shape, F32)
        return pl.pallas_call(
            functools.partial(exchange_kernel, branch, nlon, nlat),
            out_shape=(side, side, rows, jax.ShapeDtypeStruct((GROUP + 1,) + north.shape, F32)),
            in_specs=[VMEM] * 3,
            out_specs=[VMEM] * 4,
            scratch_shapes=[pltpu.SemaphoreType.DMA((5 + GROUP,)), pltpu.SemaphoreType.DMA((4 + GROUP,))],
            compiler_params=pltpu.CompilerParams(collective_id=1 + branch, has_side_effects=True),
            name=f"exchange_{branch}",
        )(cols, north, south)

    return call


def flux(c0, c1, before, after, speed, opened, diffuse):
    return opened * (speed * ((7.0 * (c0 + c1) - (before + after)) * (1.0 / 24.0)) - diffuse * (c1 - c0))


def step_kernel(
    nlon, nlat, temp, salt, u_vel, v_vel, land, partner, kappa_h, kappa_v, cols, west, east, below, above,
    temp_out, salt_out, cols_out, north_out, south_out, t_ext, s_ext, v_ext, o_ext, under, over,
):
    levels, height, _ = temp.shape
    lon, lat = lax.axis_index("lon"), lax.axis_index("lat")
    top = lat == nlat - 1
    shift = (partner[0] + lon * LANES) & (nlon * LANES - 1)
    tile, offset = shift // LANES, shift & (LANES - 1)
    near = lax.rem(tile, GROUP)
    lane_r = lax.broadcasted_iota(jnp.int32, north_out.shape, 1)
    order = jnp.where(top, (offset - lane_r) & (LANES - 1), lane_r)
    first = jnp.take_along_axis(above[jnp.where(top, near + 1, 0)], order, axis=1)
    second = jnp.take_along_axis(above[near], order, axis=1)
    over[...] = jnp.where(jnp.logical_or(jnp.logical_not(top), lane_r <= offset), first, second)
    under[...] = jnp.where(lat > 0, below[...], 0.0)
    flip = jnp.where(top, 1, 0)
    sign = jnp.where(top, -1.0, 1.0)
    end = height + 8

    def lay(l, carry):
        t_ext[l, 8:end] = temp[l]
        s_ext[l, 8:end] = salt[l]
        v_ext[l, 8:end] = v_vel[l]
        o_ext[l, 8:end] = land[l].astype(F32)
        for ref, j in ((t_ext, 0), (s_ext, 2)):
            ref[l, 6:7] = under[pl.ds(j * levels + l, 1)]
            ref[l, 7:8] = under[pl.ds((j + 1) * levels + l, 1)]
            ref[l, end : end + 1] = over[pl.ds((j + flip) * levels + l, 1)]
            ref[l, end + 1 : end + 2] = over[pl.ds((j + 1 - flip) * levels + l, 1)]
        v_ext[l, 7:8] = under[pl.ds(4 * levels + l, 1)]
        v_ext[l, end : end + 1] = over[pl.ds(4 * levels + l, 1)] * sign
        o_ext[l, 7:8] = under[pl.ds(5 * levels + l, 1)]
        o_ext[l, end : end + 1] = over[pl.ds(5 * levels + l, 1)]
        return carry

    lax.fori_loop(0, levels, lay, 0)

    lane = lax.broadcasted_iota(jnp.int32, (height, LANES), 1)
    mine, theirs, other = cols[...], west[...], east[...]
    kappas = lax.fori_loop(
        0, levels, lambda l, k: jnp.where((lane >= l * SLOT) & (lane < (l + 1) * SLOT), kappa_h[l], k), jnp.zeros_like(mine)
    )

    def west_face(back):
        def at(x, place):
            return roll(x, (LANES - place) % LANES) if place else x

        speed = at(theirs, 8 - back) + at(mine, 9 - back)
        opened = at(theirs, 10 - back) * at(mine, 11 - back)
        return flux(at(theirs, 1), at(mine, 2), theirs, at(mine, 3), speed, opened, kappas)

    faces = (west_face(0), west_face(4))

    def level(l, carry):
        base = l * SLOT
        diffuse = kappa_h[l]
        down, up = jnp.maximum(l - 1, 0), jnp.minimum(l + 1, levels - 1)
        k_down = jnp.where(l > 0, kappa_v[down], 0.0)
        k_up = jnp.where(l < levels - 1, kappa_v[jnp.minimum(l, levels - 2)], 0.0)
        own = pl.ds(8, height)
        u, o = u_vel[l], o_ext[l, own]
        u_next = jnp.where(lane == LANES - 1, roll(other, 118 - base), roll(u, LANES - 1))
        o_next = jnp.where(lane == LANES - 1, roll(other, 116 - base), roll(o, LANES - 1))
        speed_x, open_x = u + u_next, o * o_next
        tall = height + 8
        speed_y = v_ext[l, pl.ds(7, tall)] + v_ext[l, pl.ds(8, tall)]
        open_y = o_ext[l, pl.ds(7, tall)] * o_ext[l, pl.ds(8, tall)]
        lift = k_up * (o * o_ext[up, own])
        drop = k_down * (o * o_ext[down, own])
        for ext, out, face, back in ((t_ext, temp_out, faces[0], 0), (s_ext, salt_out, faces[1], 4)):
            c = ext[l, own]
            before = jnp.where(lane == 0, roll(theirs, 127 - back - base), roll(c, 1))
            next1 = jnp.where(lane == LANES - 1, roll(other, 125 - back - base), roll(c, LANES - 1))
            next2 = jnp.where(lane >= LANES - 2, roll(other, 124 - back - base), roll(c, LANES - 2))
            flux_x = flux(c, next1, before, next2, speed_x, open_x, diffuse)
            flux_w = jnp.where(lane == 0, roll(face, lax.rem(LANES - back - base + LANES, LANES)), roll(flux_x, 1))
            flux_y = flux(
                ext[l, pl.ds(7, tall)], ext[l, pl.ds(8, tall)], ext[l, pl.ds(6, tall)], ext[l, pl.ds(9, tall)],
                speed_y, open_y, diffuse,
            )
            flux_n = roll(flux_y, tall - 1, 0)
            gain = lift * (ext[up, own] - c) - drop * (c - ext[down, own])
            out[l] = c + o * (gain - (flux_x - flux_w) - (flux_n[:height] - flux_y[:height]))
        return carry

    lax.fori_loop(0, levels, level, 0)
    pack(temp_out, salt_out, u_vel, v_vel, land, cols_out, north_out, south_out)


def local(nlon, nlat, temp, salt, u_vel, v_vel, land_sea, partner, kappa_h, kappa_v):
    levels, height, width = temp.shape
    block = jax.ShapeDtypeStruct(temp.shape, F32)
    side = jax.ShapeDtypeStruct((height, width), F32)
    rows = jax.ShapeDtypeStruct((64, width), F32)
    edges = pl.pallas_call(
        pack_kernel, out_shape=(side, rows, rows), in_specs=[VMEM] * 5, out_specs=[VMEM] * 3, name="edges"
    )(temp, salt, u_vel, v_vel, land_sea)
    shift = (partner[0] + lax.axis_index("lon") * LANES) & (nlon * LANES - 1)
    branch = shift // (LANES * GROUP)
    branches = [exchange(b, nlon, nlat) for b in range(nlon // GROUP)]
    extended = pltpu.VMEM((levels, height + 24, width), F32)

    def step(i, state):
        t, s, cols, north, south = state
        west, east, below, above = lax.switch(branch, branches, cols, north, south)
        return tuple(
            pl.pallas_call(
                functools.partial(step_kernel, nlon, nlat),
                out_shape=(block, block, side, rows, rows),
                in_specs=[VMEM] * 5 + [SMEM] * 3 + [VMEM] * 5,
                out_specs=[VMEM] * 5,
                scratch_shapes=[extended] * 4 + [pltpu.VMEM((64, width), F32)] * 2,
                name="step",
            )(t, s, u_vel, v_vel, land_sea, partner, kappa_h, kappa_v, cols, west, east, below, above)
        )

    state = lax.fori_loop(0, STEPS, step, (temp, salt) + tuple(edges))
    return state[0], state[1]


def solution(mesh):
    field = P(None, "lat", "lon")
    return jax.shard_map(
        functools.partial(local, mesh.shape["lon"], mesh.shape["lat"]),
        mesh=mesh,
        in_specs=(field,) * 5 + (P("lon"), P(), P()),
        out_specs=(field, field),
        check_vma=False,
    )
```

```python
import functools

import jax
import jax.numpy as jnp
from jax import lax
from jax.experimental import pallas as pl
from jax.experimental.pallas import tpu as pltpu
from jax.sharding import PartitionSpec as P

STEPS = 2
WIDE = 8
LANES = 128
SLOT = 12
EDGE = 64
MOVING = 40
F32 = jnp.float32
MESH = pl.DeviceIdType.MESH
HALO = 8


def roll(x, shift, axis=1):
    return pltpu.roll(x, shift, axis)


def flux(c0, c1, before, after, speed, opened, diffuse):
    return opened * (speed * ((7.0 * (c0 + c1) - (before + after)) * (1.0 / 24.0)) - diffuse * (c1 - c0))


def kernel(
    nlon, nlat, temp, salt, u_vel, v_vel, land, partner, kappa_h, kappa_v, temp_out, salt_out,
    t_ext, s_ext, v_ext, o_ext, u_own, land_own, t_new, s_new, cols, north, south, relay, west, east, below, above,
    group0, group1, across0, across1, under, over, face_t, face_s,
    load_sem, out_sem, send, recv, group_send, group_recv, across_send, across_recv,
):
    group, across = (group0, group1), (across0, across1)
    levels, height, _ = temp.shape
    end = HALO + height
    lon, lat = lax.axis_index("lon"), lax.axis_index("lat")
    top = lat == nlat - 1
    right, left = lax.rem(lon + 1, nlon), lax.rem(lon + nlon - 1, nlon)
    place, far = lax.rem(lon, WIDE), lon // WIDE
    groups = nlon // WIDE

    def in_group(k):
        return far * WIDE + lax.rem(place + k, WIDE)

    def in_across(k):
        return lax.rem(far + k, groups) * WIDE + place

    loads = [
        pltpu.make_async_copy(src, dst, load_sem.at[i])
        for i, (src, dst) in enumerate(
            (
                (temp, t_ext.at[0, :, pl.ds(HALO, height)]),
                (salt, s_ext.at[0, :, pl.ds(HALO, height)]),
                (v_vel, v_ext.at[:, pl.ds(HALO, height)]),
                (land, land_own),
                (u_vel, u_own),
            )
        )
    ]
    for load in loads:
        load.start()

    barrier = pltpu.get_barrier_semaphore()

    def greet(a, b):
        pl.semaphore_signal(barrier, inc=1, device_id=(a, b), device_id_type=MESH)

    @pl.when(top)
    def _():
        for k in range(1, WIDE):
            greet(in_group(k), lat)
        for k in range(1, groups):
            greet(in_across(k), lat)

    greet(right, lat)
    greet(left, lat)

    @pl.when(lat > 0)
    def _():
        greet(lon, lat - 1)

    @pl.when(lat < nlat - 1)
    def _():
        greet(lon, lat + 1)

    expected = 2 + jnp.where(lat > 0, 1, 0) + jnp.where(top, WIDE + groups - 2, 1)

    def remote(src, dst, sent, got, a, b):
        return pltpu.make_async_remote_copy(
            src_ref=src, dst_ref=dst, send_sem=sent, recv_sem=got, device_id=(a, b), device_id_type=MESH
        )

    def rows(step):
        return pl.ds(0, EDGE if step == 0 else MOVING)

    def to_right(step):
        return remote(cols.at[step], west.at[step], send.at[step, 0], recv.at[step, 0], right, lat)

    def to_left(step):
        return remote(cols.at[step], east.at[step], send.at[step, 1], recv.at[step, 1], left, lat)

    def to_north(step):
        return remote(
            north.at[step, rows(step)], below.at[step, rows(step)], send.at[step, 2], recv.at[step, 2], lon, lax.rem(lat + 1, nlat)
        )

    def to_south(step):
        return remote(
            south.at[step, rows(step)], above.at[step, rows(step)], send.at[step, 3], recv.at[step, 3],
            lon, lax.rem(lat + nlat - 1, nlat),
        )

    def to_group(step, k):
        return remote(
            north.at[step, rows(step)], group[step].at[k, rows(step)], group_send.at[step, k], group_recv.at[step, k], in_group(k), lat
        )

    def to_across(step, k):
        return remote(
            relay.at[step, rows(step)], across[step].at[k, rows(step)], across_send.at[step, k], across_recv.at[step, k],
            in_across(k), lat,
        )

    def pack_north(step):
        def level(l, carry):
            for j, (ref, row) in enumerate(((t_ext, end - 2), (t_ext, end - 1), (s_ext, end - 2), (s_ext, end - 1))):
                north[step, pl.ds(j * levels + l, 1)] = ref[step, l, pl.ds(row, 1)]
            if step == 0:
                north[step, pl.ds(4 * levels + l, 1)] = v_ext[l, pl.ds(end - 1, 1)]
                north[step, pl.ds(5 * levels + l, 1)] = land_own[l, pl.ds(height - 1, 1)].astype(F32)
            return carry

        lax.fori_loop(0, levels, level, 0)

    def pack_south(step):
        def level(l, carry):
            for j, (ref, row) in enumerate(((t_ext, HALO), (t_ext, HALO + 1), (s_ext, HALO), (s_ext, HALO + 1))):
                south[step, pl.ds(j * levels + l, 1)] = ref[step, l, pl.ds(row, 1)]
            if step == 0:
                south[step, pl.ds(4 * levels + l, 1)] = v_ext[l, pl.ds(HALO, 1)]
                south[step, pl.ds(5 * levels + l, 1)] = land_own[l, pl.ds(0, 1)].astype(F32)
            return carry

        lax.fori_loop(0, levels, level, 0)

    lane = lax.broadcasted_iota(jnp.int32, (height, LANES), 1)
    own = pl.ds(HALO, height)

    def pack_cols(step):
        def level(l, held):
            base = l * SLOT
            here = lane - base
            held = jnp.where((here >= 0) & (here < 4), roll(t_ext[step, l, own], base + 2), held)
            held = jnp.where((here >= 4) & (here < 8), roll(s_ext[step, l, own], base + 6), held)
            held = jnp.where((here >= 8) & (here < 10), roll(u_own[l], base + 9), held)
            return jnp.where((here >= 10) & (here < 12), roll(o_ext[l, own], base + 11), held)

        cols[step] = lax.fori_loop(0, levels, level, jnp.zeros((height, LANES), F32))

    def lay_south(step):
        under[...] = jnp.where(lat > 0, below[step], 0.0)

        def level(l, carry):
            for ref, j in ((t_ext, 0), (s_ext, 2)):
                ref[step, l, pl.ds(HALO - 2, 1)] = under[pl.ds(j * levels + l, 1)]
                ref[step, l, pl.ds(HALO - 1, 1)] = under[pl.ds((j + 1) * levels + l, 1)]
            if step == 0:
                v_ext[l, pl.ds(HALO - 1, 1)] = under[pl.ds(4 * levels + l, 1)]
                o_ext[l, pl.ds(HALO - 1, 1)] = under[pl.ds(5 * levels + l, 1)]
            return carry

        lax.fori_loop(0, levels, level, 0)

    def lay_north(step, source, folded):
        flip, sign = (1, -1.0) if folded else (0, 1.0)

        def level(l, carry):
            for ref, j in ((t_ext, 0), (s_ext, 2)):
                ref[step, l, pl.ds(end, 1)] = source[pl.ds((j + flip) * levels + l, 1)]
                ref[step, l, pl.ds(end + 1, 1)] = source[pl.ds((j + 1 - flip) * levels + l, 1)]
            if step == 0:
                v_ext[l, pl.ds(end, 1)] = source[pl.ds(4 * levels + l, 1)] * sign
                o_ext[l, pl.ds(end, 1)] = source[pl.ds(5 * levels + l, 1)]
            return carry

        lax.fori_loop(0, levels, level, 0)

    def make_faces(step):
        mine, theirs = cols[step], west[step]
        kappas = lax.fori_loop(
            0,
            levels,
            lambda l, k: jnp.where((lane >= l * SLOT) & (lane < (l + 1) * SLOT), kappa_h[l], k),
            jnp.zeros((height, LANES), F32),
        )

        def at(x, p):
            return roll(x, (LANES - p) % LANES) if p else x

        for ref, back in ((face_t, 0), (face_s, 4)):
            speed = at(theirs, 8 - back) + at(mine, 9 - back)
            opened = at(theirs, 10 - back) * at(mine, 11 - back)
            ref[...] = flux(at(theirs, 1), at(mine, 2), theirs, at(mine, 3), speed, opened, kappas)

    def advance(step, row, count, t_out, s_out, shift):
        here, tall = pl.ds(HALO + row, count), count + 8
        span = lane[:count]
        side = pl.ds(row, count)
        theirs, other = west[step, side], east[step, side]
        faces = (face_t[side], face_s[side])

        def rise(k):
            return pl.ds(HALO + row - 1 + k, tall)

        def level(l, carry):
            base = l * SLOT
            diffuse = kappa_h[l]
            down, up = jnp.maximum(l - 1, 0), jnp.minimum(l + 1, levels - 1)
            k_down = jnp.where(l > 0, kappa_v[down], 0.0)
            k_up = jnp.where(l < levels - 1, kappa_v[jnp.minimum(l, levels - 2)], 0.0)
            u, o = u_own[l, side], o_ext[l, here]
            u_next = jnp.where(span == LANES - 1, roll(other, 118 - base), roll(u, LANES - 1))
            o_next = jnp.where(span == LANES - 1, roll(other, 116 - base), roll(o, LANES - 1))
            speed_x, open_x = u + u_next, o * o_next
            speed_y = v_ext[l, rise(0)] + v_ext[l, rise(1)]
            open_y = o_ext[l, rise(0)] * o_ext[l, rise(1)]
            lift = k_up * (o * o_ext[up, here])
            drop = k_down * (o * o_ext[down, here])
            for ext, out, face, back in ((t_ext, t_out, faces[0], 0), (s_ext, s_out, faces[1], 4)):
                c = ext[step, l, here]
                before = jnp.where(span == 0, roll(theirs, 127 - back - base), roll(c, 1))
                next1 = jnp.where(span == LANES - 1, roll(other, 125 - back - base), roll(c, LANES - 1))
                next2 = jnp.where(span >= LANES - 2, roll(other, 124 - back - base), roll(c, LANES - 2))
                flux_x = flux(c, next1, before, next2, speed_x, open_x, diffuse)
                flux_w = jnp.where(span == 0, roll(face, lax.rem(2 * LANES - back - base, LANES)), roll(flux_x, 1))
                flux_y = flux(
                    ext[step, l, rise(0)], ext[step, l, rise(1)], ext[step, l, rise(-1)], ext[step, l, rise(2)],
                    speed_y, open_y, diffuse,
                )
                flux_n = roll(flux_y, tall - 1, 0)
                gain = lift * (ext[step, up, here] - c) - drop * (c - ext[step, down, here])
                out[l, pl.ds(shift + row, count)] = c + o * (
                    gain - (flux_x - flux_w) - (flux_n[:count] - flux_y[:count])
                )
            return carry

        lax.fori_loop(0, levels, level, 0)

    shift = (partner[0] + lon * LANES) & (nlon * LANES - 1)
    tile, offset = shift // LANES, shift & (LANES - 1)
    tile_far, tile_place = tile // WIDE, lax.rem(tile, WIDE)
    edge_lane = lax.broadcasted_iota(jnp.int32, (EDGE, LANES), 1)
    order = (offset - edge_lane) & (LANES - 1)
    near_part = edge_lane <= offset
    borrow0 = jnp.where(tile_place < place, 1, 0)
    borrow1 = jnp.where(tile_place - 1 < place, 1, 0)

    def assemble(step):
        first = jnp.take_along_axis(group[step][lax.rem(2 * place - tile_place + WIDE, WIDE)], order, axis=1)
        second = jnp.take_along_axis(group[step][lax.rem(2 * place - tile_place + 1 + WIDE, WIDE)], order, axis=1)
        relay[step] = jnp.where(near_part, first, second)

    def choose(step):
        from0 = across[step][lax.rem(2 * far - tile_far + borrow0 + 2 * groups, groups)]
        from1 = across[step][lax.rem(2 * far - tile_far + borrow1 + 2 * groups, groups)]
        over[...] = jnp.where(near_part, from0, from1)

    for load in loads[:4]:
        load.wait()
    pack_north(0)
    pack_south(0)
    pl.semaphore_wait(barrier, expected)

    @pl.when(top)
    def _():
        for k in range(1, WIDE):
            to_group(0, k).start()
        group[0][0] = north[0]

    @pl.when(lat < nlat - 1)
    def _():
        to_north(0).start()

    @pl.when(lat > 0)
    def _():
        to_south(0).start()

    loads[4].wait()

    def ocean(l, carry):
        o_ext[l, own] = land_own[l].astype(F32)
        return carry

    lax.fori_loop(0, levels, ocean, 0)

    for step in range(STEPS):
        last = step == STEPS - 1
        t_out, s_out, at = (t_new, s_new, 0) if last else (t_ext.at[step + 1], s_ext.at[step + 1], HALO)
        pack_cols(step)
        to_right(step).start()
        to_left(step).start()

        @pl.when(top)
        def _():
            for k in range(1, WIDE):
                to_group(step, k).wait_recv()
            assemble(step)
            for k in range(1, groups):
                to_across(step, k).start()
            across[step][0] = relay[step]

        @pl.when(lat > 0)
        def _():
            to_north(step).wait_recv()

        lay_south(step)

        @pl.when(lat < nlat - 1)
        def _():
            to_south(step).wait_recv()
            lay_north(step, above.at[step], False)

        to_right(step).wait_recv()
        to_left(step).wait_recv()
        make_faces(step)
        advance(step, 0, height, t_out, s_out, at)
        if not last:
            pack_south(step + 1)

            @pl.when(lat > 0)
            def _():
                to_south(step + 1).start()

        @pl.when(top)
        def _():
            for k in range(1, groups):
                to_across(step, k).wait_recv()
            choose(step)
            lay_north(step, over, True)
            advance(step, height - 8, 8, t_out, s_out, at)

        if not last:
            pack_north(step + 1)

            @pl.when(top)
            def _():
                for k in range(1, WIDE):
                    to_group(step + 1, k).start()
                group[step + 1][0] = north[step + 1]

            @pl.when(lat < nlat - 1)
            def _():
                to_north(step + 1).start()

    outs = [
        pltpu.make_async_copy(src, dst, out_sem.at[i]) for i, (src, dst) in enumerate(((t_new, temp_out), (s_new, salt_out)))
    ]
    for out in outs:
        out.start()
    for step in range(STEPS):
        to_right(step).wait_send()
        to_left(step).wait_send()

        @pl.when(lat < nlat - 1)
        def _():
            to_north(step).wait_send()

        @pl.when(lat > 0)
        def _():
            to_south(step).wait_send()

        @pl.when(top)
        def _():
            for k in range(1, WIDE):
                to_group(step, k).wait_send()
            for k in range(1, groups):
                to_across(step, k).wait_send()

    for out in outs:
        out.wait()


def local(nlon, nlat, temp, salt, u_vel, v_vel, land_sea, partner, kappa_h, kappa_v):
    levels, height, width = temp.shape
    block = jax.ShapeDtypeStruct(temp.shape, F32)
    anywhere = pl.BlockSpec(memory_space=pl.ANY)
    numbers = pl.BlockSpec(memory_space=pltpu.SMEM)
    groups = nlon // WIDE

    def room(*shape):
        return pltpu.VMEM(shape, F32)

    tall = height + 24
    return pl.pallas_call(
        functools.partial(kernel, nlon, nlat),
        out_shape=(block, block),
        in_specs=[anywhere] * 5 + [numbers] * 3,
        out_specs=[anywhere] * 2,
        scratch_shapes=[
            room(STEPS, levels, tall, width),
            room(STEPS, levels, tall, width),
            room(levels, tall, width),
            room(levels, tall, width),
            room(levels, height, width),
            pltpu.VMEM((levels, height, width), jnp.int32),
            room(levels, height, width),
            room(levels, height, width),
            room(STEPS, height, width),
            room(STEPS, EDGE, width),
            room(STEPS, EDGE, width),
            room(STEPS, EDGE, width),
            room(STEPS, height, width),
            room(STEPS, height, width),
            room(STEPS, EDGE, width),
            room(STEPS, EDGE, width),
            room(WIDE, EDGE, width),
            room(WIDE, EDGE, width),
            room(groups, EDGE, width),
            room(groups, EDGE, width),
            room(EDGE, width),
            room(EDGE, width),
            room(height, width),
            room(height, width),
            pltpu.SemaphoreType.DMA((5,)),
            pltpu.SemaphoreType.DMA((2,)),
            pltpu.SemaphoreType.DMA((STEPS, 4)),
            pltpu.SemaphoreType.DMA((STEPS, 4)),
            pltpu.SemaphoreType.DMA((STEPS, WIDE)),
            pltpu.SemaphoreType.DMA((STEPS, WIDE)),
            pltpu.SemaphoreType.DMA((STEPS, groups)),
            pltpu.SemaphoreType.DMA((STEPS, groups)),
        ],
        compiler_params=pltpu.CompilerParams(collective_id=0, has_side_effects=True, vmem_limit_bytes=60 << 20),
        name="tracer_steps",
    )(temp, salt, u_vel, v_vel, land_sea, partner, kappa_h, kappa_v)


def solution(mesh):
    field = P(None, "lat", "lon")
    return jax.shard_map(
        functools.partial(local, mesh.shape["lon"], mesh.shape["lat"]),
        mesh=mesh,
        in_specs=(field,) * 5 + (P("lon"), P(), P()),
        out_specs=(field, field),
        check_vma=False,
    )
```

```python
import functools

import jax
import jax.numpy as jnp
from jax import lax
from jax.experimental import pallas as pl
from jax.experimental.pallas import tpu as pltpu
from jax.sharding import PartitionSpec as P

STEPS = 2
WIDE = 8
LANES = 128
SLOT = 12
EDGE = 32
UNROLL = 5
F32 = jnp.float32
MESH = pl.DeviceIdType.MESH
HALO = 8


def roll(x, shift, axis=1):
    return pltpu.roll(x, shift, axis)


def flux(c0, c1, before, after, speed, opened, diffuse):
    return opened * (speed * ((7.0 * (c0 + c1) - (before + after)) * (1.0 / 24.0)) - diffuse * (c1 - c0))


def kernel(
    nlon, nlat, temp, salt, u_vel, v_vel, land, partner, kappa_h, kappa_v, temp_out, salt_out,
    t_ext, s_ext, v_ext, o_ext, u_own, land_own, land_rows, cols, north, south, relay, west, east, below, above,
    near00, near01, near10, near11, far00, far01, far10, far11, under, over, face_t, face_s,
    load_sem, row_sem, send, recv, near_send, near_recv, far_send, far_recv,
):
    hop_near, hop_far = ((near00, near01), (near10, near11)), ((far00, far01), (far10, far11))
    levels, height, _ = temp.shape
    end = HALO + height
    lon, lat = lax.axis_index("lon"), lax.axis_index("lat")
    top = lat == nlat - 1
    right, left = lax.rem(lon + 1, nlon), lax.rem(lon + nlon - 1, nlon)
    place, far = lax.rem(lon, WIDE), lon // WIDE
    groups = nlon // WIDE

    def farthest_first(count):
        return sorted(range(1, count), key=lambda k: -min(k, count - k))

    def in_group(k):
        return far * WIDE + lax.rem(place + k, WIDE)

    def in_across(k):
        return lax.rem(far + k, groups) * WIDE + place

    def row_copy(field, row, dst, i):
        return pltpu.make_async_copy(field.at[:, row], dst, row_sem.at[i])

    first_rows = [
        row_copy(temp, height - 2, north.at[0, 0, pl.ds(0, levels)], 0),
        row_copy(temp, height - 1, north.at[0, 0, pl.ds(levels, levels)], 1),
        row_copy(v_vel, height - 1, north.at[0, 0, pl.ds(2 * levels, levels)], 2),
        row_copy(salt, height - 2, north.at[0, 1, pl.ds(0, levels)], 3),
        row_copy(salt, height - 1, north.at[0, 1, pl.ds(levels, levels)], 4),
        row_copy(land, height - 1, land_rows.at[0], 5),
        row_copy(temp, 0, south.at[0, 0, pl.ds(0, levels)], 6),
        row_copy(temp, 1, south.at[0, 0, pl.ds(levels, levels)], 7),
        row_copy(v_vel, 0, south.at[0, 0, pl.ds(2 * levels, levels)], 8),
        row_copy(salt, 0, south.at[0, 1, pl.ds(0, levels)], 9),
        row_copy(salt, 1, south.at[0, 1, pl.ds(levels, levels)], 10),
        row_copy(land, 0, land_rows.at[1], 11),
    ]
    for copy in first_rows:
        copy.start()

    loads = [
        pltpu.make_async_copy(src, dst, load_sem.at[i])
        for i, (src, dst) in enumerate(
            (
                (temp, t_ext.at[0, :, pl.ds(HALO, height)]),
                (salt, s_ext.at[0, :, pl.ds(HALO, height)]),
                (v_vel, v_ext.at[:, pl.ds(HALO, height)]),
                (land, land_own),
                (u_vel, u_own),
            )
        )
    ]
    for load in loads:
        load.start()

    barrier = pltpu.get_barrier_semaphore()

    def greet(a, b):
        pl.semaphore_signal(barrier, inc=1, device_id=(a, b), device_id_type=MESH)

    @pl.when(top)
    def _():
        for k in range(1, WIDE):
            greet(in_group(k), lat)
        for k in range(1, groups):
            greet(in_across(k), lat)

    greet(right, lat)
    greet(left, lat)

    @pl.when(lat > 0)
    def _():
        greet(lon, lat - 1)

    @pl.when(lat < nlat - 1)
    def _():
        greet(lon, lat + 1)

    expected = 2 + jnp.where(lat > 0, 1, 0) + jnp.where(top, WIDE + groups - 2, 1)

    def remote(src, dst, sent, got, a, b):
        return pltpu.make_async_remote_copy(
            src_ref=src, dst_ref=dst, send_sem=sent, recv_sem=got, device_id=(a, b), device_id_type=MESH
        )

    def rows(step):
        return pl.ds(0, (3 if step == 0 else 2) * levels)

    def to_right(step):
        return remote(cols.at[step], west.at[step], send.at[step, 0], recv.at[step, 0], right, lat)

    def to_left(step):
        return remote(cols.at[step], east.at[step], send.at[step, 1], recv.at[step, 1], left, lat)

    def to_north(step):
        return remote(
            north.at[step, :, rows(step)], below.at[step, :, rows(step)], send.at[step, 2], recv.at[step, 2],
            lon, lax.rem(lat + 1, nlat),
        )

    def to_south(step):
        return remote(
            south.at[step, :, rows(step)], above.at[step, :, rows(step)], send.at[step, 3], recv.at[step, 3],
            lon, lax.rem(lat + nlat - 1, nlat),
        )

    def hop(step, tracer, near, k):
        message = (north if near == (tracer == 0) else relay).at[step, tracer, rows(step)]
        slots, sent, got, to = (
            (hop_near, near_send, near_recv, in_group) if near else (hop_far, far_send, far_recv, in_across)
        )
        return remote(
            message, slots[step][tracer].at[k, rows(step)], sent.at[step, tracer, k], got.at[step, tracer, k], to(k), lat
        )

    def peers(near):
        return farthest_first(WIDE if near else groups)

    def first_hop(step):
        for k in range(max(WIDE, groups)):
            for tracer, near in ((0, True), (1, False)):
                if k < len(peers(near)):
                    hop(step, tracer, near, peers(near)[k]).start()
        hop_near[step][0][0] = north[step, 0]
        hop_far[step][1][0] = north[step, 1]

    def pack_rows(step, ref, row):
        def level(l, carry):
            for tracer, ext in enumerate((t_ext, s_ext)):
                for i in range(2):
                    ref[step, tracer, pl.ds(i * levels + l, 1)] = ext[step, l, pl.ds(row + i, 1)]
            return carry

        lax.fori_loop(0, levels, level, 0, unroll=UNROLL)

    lane = lax.broadcasted_iota(jnp.int32, (height, LANES), 1)
    own = pl.ds(HALO, height)

    def pack_cols(step):
        def level(l, held):
            base = l * SLOT
            here = lane - base
            held = jnp.where((here >= 0) & (here < 4), roll(t_ext[step, l, own], base + 2), held)
            held = jnp.where((here >= 4) & (here < 8), roll(s_ext[step, l, own], base + 6), held)
            held = jnp.where((here >= 8) & (here < 10), roll(u_own[l], base + 9), held)
            return jnp.where((here >= 10) & (here < 12), roll(o_ext[l, own], base + 11), held)

        cols[step] = lax.fori_loop(0, levels, level, jnp.zeros((height, LANES), F32), unroll=UNROLL)

    def lay(step, source, row, still, flip, sign):
        def level(l, carry):
            for tracer, ext in enumerate((t_ext, s_ext)):
                ext[step, l, pl.ds(row, 1)] = source[tracer, pl.ds(flip * levels + l, 1)]
                ext[step, l, pl.ds(row + 1, 1)] = source[tracer, pl.ds((1 - flip) * levels + l, 1)]
            if step == 0:
                v_ext[l, pl.ds(still, 1)] = source[0, pl.ds(2 * levels + l, 1)] * sign
                o_ext[l, pl.ds(still, 1)] = source[1, pl.ds(2 * levels + l, 1)]
            return carry

        lax.fori_loop(0, levels, level, 0, unroll=UNROLL)

    def lay_south(step):
        under[...] = jnp.where(lat > 0, below[step], 0.0)
        lay(step, under, HALO - 2, HALO - 1, 0, 1.0)

    def lay_north(step, source, folded):
        lay(step, source, end, end, 1 if folded else 0, -1.0 if folded else 1.0)

    def make_faces(step):
        mine, theirs = cols[step], west[step]
        kappas = lax.fori_loop(
            0,
            levels,
            lambda l, k: jnp.where((lane >= l * SLOT) & (lane < (l + 1) * SLOT), kappa_h[l], k),
            jnp.zeros((height, LANES), F32),
        )

        def at(x, p):
            return roll(x, (LANES - p) % LANES) if p else x

        for ref, back in ((face_t, 0), (face_s, 4)):
            speed = at(theirs, 8 - back) + at(mine, 9 - back)
            opened = at(theirs, 10 - back) * at(mine, 11 - back)
            ref[...] = flux(at(theirs, 1), at(mine, 2), theirs, at(mine, 3), speed, opened, kappas)

    def advance(step, row, count, t_out, s_out, shift):
        here, tall = pl.ds(HALO + row, count), count + 8
        span = lane[:count]
        side = pl.ds(row, count)
        theirs, other = west[step, side], east[step, side]
        faces = (face_t[side], face_s[side])

        def rise(k):
            return pl.ds(HALO + row - 1 + k, tall)

        def level(l, carry):
            base = l * SLOT
            diffuse = kappa_h[l]
            down, up = jnp.maximum(l - 1, 0), jnp.minimum(l + 1, levels - 1)
            k_down = jnp.where(l > 0, kappa_v[down], 0.0)
            k_up = jnp.where(l < levels - 1, kappa_v[jnp.minimum(l, levels - 2)], 0.0)
            u, o = u_own[l, side], o_ext[l, here]
            u_next = jnp.where(span == LANES - 1, roll(other, 118 - base), roll(u, LANES - 1))
            o_next = jnp.where(span == LANES - 1, roll(other, 116 - base), roll(o, LANES - 1))
            speed_x, open_x = u + u_next, o * o_next
            speed_y = v_ext[l, rise(0)] + v_ext[l, rise(1)]
            open_y = o_ext[l, rise(0)] * o_ext[l, rise(1)]
            lift = k_up * (o * o_ext[up, here])
            drop = k_down * (o * o_ext[down, here])
            for ext, out, face, back in ((t_ext, t_out, faces[0], 0), (s_ext, s_out, faces[1], 4)):
                c = ext[step, l, here]
                before = jnp.where(span == 0, roll(theirs, 127 - back - base), roll(c, 1))
                next1 = jnp.where(span == LANES - 1, roll(other, 125 - back - base), roll(c, LANES - 1))
                next2 = jnp.where(span >= LANES - 2, roll(other, 124 - back - base), roll(c, LANES - 2))
                flux_x = flux(c, next1, before, next2, speed_x, open_x, diffuse)
                flux_w = jnp.where(span == 0, roll(face, lax.rem(2 * LANES - back - base, LANES)), roll(flux_x, 1))
                flux_y = flux(
                    ext[step, l, rise(0)], ext[step, l, rise(1)], ext[step, l, rise(-1)], ext[step, l, rise(2)],
                    speed_y, open_y, diffuse,
                )
                flux_n = roll(flux_y, tall - 1, 0)
                gain = lift * (ext[step, up, here] - c) - drop * (c - ext[step, down, here])
                out[l, pl.ds(shift + row, count)] = c + o * (
                    gain - (flux_x - flux_w) - (flux_n[:count] - flux_y[:count])
                )
            return carry

        lax.fori_loop(0, levels, level, 0, unroll=UNROLL)

    shift = (partner[0] + lon * LANES) & (nlon * LANES - 1)
    tile, offset = shift // LANES, shift & (LANES - 1)
    tile_far, tile_place = tile // WIDE, lax.rem(tile, WIDE)
    edge_lane = lax.broadcasted_iota(jnp.int32, (EDGE, LANES), 1)
    order = (offset - edge_lane) & (LANES - 1)
    near_part = edge_lane <= offset
    borrow0 = jnp.where(tile_place < place, 1, 0)
    borrow1 = jnp.where(tile_place - 1 < place, 1, 0)

    near_slots = [lax.rem(2 * place - tile_place + i + WIDE, WIDE) for i in range(2)]
    far_slots = [lax.rem(2 * far - tile_far + borrow + 2 * groups, groups) for borrow in (borrow0, borrow1)]

    def wait_hop(step, tracer, near):
        for k in peers(near):
            hop(step, tracer, near, k).wait_recv()

    def picked(step, tracer, near):
        slots, at = (hop_near, near_slots) if near else (hop_far, far_slots)
        return slots[step][tracer][at[0]], slots[step][tracer][at[1]]

    def second_hop(step):
        for tracer, near in ((0, True), (1, False)):
            wait_hop(step, tracer, near)
            first, second = picked(step, tracer, near)
            first = jnp.take_along_axis(first, order, axis=1)
            second = jnp.take_along_axis(second, order, axis=1)
            relay[step, tracer] = jnp.where(near_part, first, second)
            for k in peers(not near):
                hop(step, tracer, not near, k).start()
            (hop_far if near else hop_near)[step][tracer][0] = relay[step, tracer]

    def choose(step):
        for tracer, near in ((0, False), (1, True)):
            wait_hop(step, tracer, near)
            first, second = picked(step, tracer, near)
            over[tracer] = jnp.where(near_part, first, second)

    for copy in first_rows[:6]:
        copy.wait()
    north[0, 1, pl.ds(2 * levels, levels)] = land_rows[0].astype(F32)
    pl.semaphore_wait(barrier, expected)

    @pl.when(top)
    def _():
        first_hop(0)

    @pl.when(lat < nlat - 1)
    def _():
        to_north(0).start()

    for copy in first_rows[6:]:
        copy.wait()
    south[0, 1, pl.ds(2 * levels, levels)] = land_rows[1].astype(F32)

    @pl.when(lat > 0)
    def _():
        to_south(0).start()

    for load in loads:
        load.wait()

    def ocean(l, carry):
        o_ext[l, own] = land_own[l].astype(F32)
        return carry

    lax.fori_loop(0, levels, ocean, 0, unroll=UNROLL)

    for step in range(STEPS):
        last = step == STEPS - 1
        t_out, s_out, at = (temp_out, salt_out, 0) if last else (t_ext.at[step + 1], s_ext.at[step + 1], HALO)
        pack_cols(step)
        to_right(step).start()
        to_left(step).start()

        @pl.when(top)
        def _():
            second_hop(step)

        @pl.when(lat > 0)
        def _():
            to_north(step).wait_recv()

        lay_south(step)

        @pl.when(lat < nlat - 1)
        def _():
            to_south(step).wait_recv()
            lay_north(step, above.at[step], False)

        to_right(step).wait_recv()
        to_left(step).wait_recv()
        make_faces(step)
        advance(step, 0, height, t_out, s_out, at)
        if not last:
            pack_rows(step + 1, south, HALO)

            @pl.when(lat > 0)
            def _():
                to_south(step + 1).start()

        @pl.when(top)
        def _():
            choose(step)
            lay_north(step, over, True)
            advance(step, height - 8, 8, t_out, s_out, at)

        if not last:
            pack_rows(step + 1, north, end - 2)

            @pl.when(top)
            def _():
                first_hop(step + 1)

            @pl.when(lat < nlat - 1)
            def _():
                to_north(step + 1).start()

    for step in range(STEPS):
        to_right(step).wait_send()
        to_left(step).wait_send()

        @pl.when(lat < nlat - 1)
        def _():
            to_north(step).wait_send()

        @pl.when(lat > 0)
        def _():
            to_south(step).wait_send()

        @pl.when(top)
        def _():
            for tracer in range(2):
                for near in (True, False):
                    for k in peers(near):
                        hop(step, tracer, near, k).wait_send()


def local(nlon, nlat, temp, salt, u_vel, v_vel, land_sea, partner, kappa_h, kappa_v):
    levels, height, width = temp.shape
    block = jax.ShapeDtypeStruct(temp.shape, F32)
    anywhere = pl.BlockSpec(memory_space=pl.ANY)
    numbers = pl.BlockSpec(memory_space=pltpu.SMEM)
    groups = nlon // WIDE

    def room(*shape):
        return pltpu.VMEM(shape, F32)

    tall = height + 24
    return pl.pallas_call(
        functools.partial(kernel, nlon, nlat),
        out_shape=(block, block),
        in_specs=[anywhere] * 5 + [numbers] * 3,
        out_specs=[pl.BlockSpec(memory_space=pltpu.VMEM)] * 2,
        scratch_shapes=[
            room(STEPS, levels, tall, width),
            room(STEPS, levels, tall, width),
            room(levels, tall, width),
            room(levels, tall, width),
            room(levels, height, width),
            pltpu.VMEM((levels, height, width), jnp.int32),
            pltpu.VMEM((2, levels, width), jnp.int32),
            room(STEPS, height, width),
            room(STEPS, 2, EDGE, width),
            room(STEPS, 2, EDGE, width),
            room(STEPS, 2, EDGE, width),
            room(STEPS, height, width),
            room(STEPS, height, width),
            room(STEPS, 2, EDGE, width),
            room(STEPS, 2, EDGE, width),
            *[room(WIDE, EDGE, width)] * (2 * STEPS),
            *[room(groups, EDGE, width)] * (2 * STEPS),
            room(2, EDGE, width),
            room(2, EDGE, width),
            room(height, width),
            room(height, width),
            pltpu.SemaphoreType.DMA((5,)),
            pltpu.SemaphoreType.DMA((12,)),
            pltpu.SemaphoreType.DMA((STEPS, 4)),
            pltpu.SemaphoreType.DMA((STEPS, 4)),
            pltpu.SemaphoreType.DMA((STEPS, 2, WIDE)),
            pltpu.SemaphoreType.DMA((STEPS, 2, WIDE)),
            pltpu.SemaphoreType.DMA((STEPS, 2, groups)),
            pltpu.SemaphoreType.DMA((STEPS, 2, groups)),
        ],
        compiler_params=pltpu.CompilerParams(collective_id=0, has_side_effects=True, vmem_limit_bytes=60 << 20),
        name="tracer_steps",
    )(temp, salt, u_vel, v_vel, land_sea, partner, kappa_h, kappa_v)


def solution(mesh):
    field = P(None, "lat", "lon")
    return jax.shard_map(
        functools.partial(local, mesh.shape["lon"], mesh.shape["lat"]),
        mesh=mesh,
        in_specs=(field,) * 5 + (P("lon"), P(), P()),
        out_specs=(field, field),
        check_vma=False,
    )
```

```python
import functools

import jax
import jax.numpy as jnp
from jax import lax
from jax.experimental import pallas as pl
from jax.experimental.pallas import tpu as pltpu
from jax.sharding import PartitionSpec as P

STEPS = 2
WIDE = 8
LANES = 128
SLOT = 12
EDGE = 32
UNROLL = 5
F32 = jnp.float32
MESH = pl.DeviceIdType.MESH
HALO = 8


def roll(x, shift, axis=1):
    return pltpu.roll(x, shift, axis)


def flux(c0, c1, before, after, speed, opened, diffuse):
    return opened * (speed * ((7.0 * (c0 + c1) - (before + after)) * (1.0 / 24.0)) - diffuse * (c1 - c0))


def kernel(
    nlon, nlat, temp, salt, u_vel, v_vel, land, partner_in, kappa_h_in, kappa_v_in, temp_out, salt_out,
    partner, kappa_h, kappa_v,
    t_ext, s_ext, v_ext, o_ext, u_own, land_own, land_rows, cols, north, south, relay, west, east, below, above,
    near00, near01, near10, near11, far00, far01, far10, far11, under, over, under_top, mending,
    face_t, face_s, kappas,
    load_sem, row_sem, send, recv, near_send, near_recv, far_send, far_recv,
):
    hop_near, hop_far = ((near00, near01), (near10, near11)), ((far00, far01), (far10, far11))
    levels, height, _ = temp.shape
    end = HALO + height
    lon, lat = lax.axis_index("lon"), lax.axis_index("lat")
    top = lat == nlat - 1
    right, left = lax.rem(lon + 1, nlon), lax.rem(lon + nlon - 1, nlon)
    place, far = lax.rem(lon, WIDE), lon // WIDE
    groups = nlon // WIDE

    def farthest_first(count):
        return sorted(range(1, count), key=lambda k: -min(k, count - k))

    def in_group(k):
        return far * WIDE + lax.rem(place + k, WIDE)

    def in_across(k):
        return lax.rem(far + k, groups) * WIDE + place

    def row_copy(field, row, dst, i):
        return pltpu.make_async_copy(field.at[:, row], dst, row_sem.at[i])

    first_rows = [
        row_copy(temp, height - 2, north.at[0, 0, pl.ds(0, levels)], 0),
        row_copy(temp, height - 1, north.at[0, 0, pl.ds(levels, levels)], 1),
        row_copy(v_vel, height - 1, north.at[0, 0, pl.ds(2 * levels, levels)], 2),
        row_copy(salt, height - 2, north.at[0, 1, pl.ds(0, levels)], 3),
        row_copy(salt, height - 1, north.at[0, 1, pl.ds(levels, levels)], 4),
        row_copy(land, height - 1, land_rows.at[0], 5),
        row_copy(temp, 0, south.at[0, 0, pl.ds(0, levels)], 6),
        row_copy(temp, 1, south.at[0, 0, pl.ds(levels, levels)], 7),
        row_copy(v_vel, 0, south.at[0, 0, pl.ds(2 * levels, levels)], 8),
        row_copy(salt, 0, south.at[0, 1, pl.ds(0, levels)], 9),
        row_copy(salt, 1, south.at[0, 1, pl.ds(levels, levels)], 10),
        row_copy(land, 0, land_rows.at[1], 11),
    ]
    loads = [
        pltpu.make_async_copy(src, dst, load_sem.at[i])
        for i, (src, dst) in enumerate(
            (
                (temp, t_ext.at[0, :, pl.ds(HALO, height)]),
                (salt, s_ext.at[0, :, pl.ds(HALO, height)]),
                (v_vel, v_ext.at[:, pl.ds(HALO, height)]),
                (land, land_own),
                (u_vel, u_own),
                (partner_in, partner),
                (kappa_h_in, kappa_h),
                (kappa_v_in, kappa_v),
            )
        )
    ]
    barrier = pltpu.get_barrier_semaphore()

    def greet(a, b):
        pl.semaphore_signal(barrier, inc=1, device_id=(a, b), device_id_type=MESH)

    @pl.when(top)
    def _():
        for k in range(1, WIDE):
            greet(in_group(k), lat)
        for k in range(1, groups):
            greet(in_across(k), lat)

    greet(right, lat)
    greet(left, lat)

    @pl.when(lat > 0)
    def _():
        greet(lon, lat - 1)

    @pl.when(lat < nlat - 1)
    def _():
        greet(lon, lat + 1)

    expected = 2 + jnp.where(lat > 0, 1, 0) + jnp.where(top, WIDE + groups - 2, 1)

    for copy in first_rows + loads:
        copy.start()

    def remote(src, dst, sent, got, a, b):
        return pltpu.make_async_remote_copy(
            src_ref=src, dst_ref=dst, send_sem=sent, recv_sem=got, device_id=(a, b), device_id_type=MESH
        )

    def rows(step):
        return pl.ds(0, (3 if step == 0 else 2) * levels)

    def to_right(step):
        return remote(cols.at[step], west.at[step], send.at[step, 0], recv.at[step, 0], right, lat)

    def to_left(step):
        return remote(cols.at[step], east.at[step], send.at[step, 1], recv.at[step, 1], left, lat)

    def to_north(step):
        return remote(
            north.at[step, :, rows(step)], below.at[step, :, rows(step)], send.at[step, 2], recv.at[step, 2],
            lon, lax.rem(lat + 1, nlat),
        )

    def to_south(step):
        return remote(
            south.at[step, :, rows(step)], above.at[step, :, rows(step)], send.at[step, 3], recv.at[step, 3],
            lon, lax.rem(lat + nlat - 1, nlat),
        )

    def hop(step, tracer, near, k):
        message = (north if near == (tracer == 0) else relay).at[step, tracer, rows(step)]
        slots, sent, got, to = (
            (hop_near, near_send, near_recv, in_group) if near else (hop_far, far_send, far_recv, in_across)
        )
        return remote(
            message, slots[step][tracer].at[k, rows(step)], sent.at[step, tracer, k], got.at[step, tracer, k], to(k), lat
        )

    def peers(near):
        return farthest_first(WIDE if near else groups)

    def first_hop(step):
        for k in range(max(WIDE, groups)):
            for tracer, near in ((0, True), (1, False)):
                if k < len(peers(near)):
                    hop(step, tracer, near, peers(near)[k]).start()
        hop_near[step][0][0] = north[step, 0]
        hop_far[step][1][0] = north[step, 1]

    def pack_rows(step, ref, row):
        def level(l, carry):
            for tracer, ext in enumerate((t_ext, s_ext)):
                for i in range(2):
                    ref[step, tracer, pl.ds(i * levels + l, 1)] = ext[step, l, pl.ds(row + i, 1)]
            return carry

        lax.fori_loop(0, levels, level, 0, unroll=UNROLL)

    lane = lax.broadcasted_iota(jnp.int32, (height, LANES), 1)
    own = pl.ds(HALO, height)

    def pack_cols(step):
        def level(l, held):
            base = l * SLOT
            here = lane - base
            held = jnp.where((here >= 0) & (here < 4), roll(t_ext[step, l, own], base + 2), held)
            held = jnp.where((here >= 4) & (here < 8), roll(s_ext[step, l, own], base + 6), held)
            if step == 0:
                held = jnp.where((here >= 8) & (here < 10), roll(u_own[l], base + 9), held)
                held = jnp.where((here >= 10) & (here < 12), roll(o_ext[l, own], base + 11), held)
            return held

        cols[step] = lax.fori_loop(0, levels, level, cols[0] if step else jnp.zeros((height, LANES), F32), unroll=UNROLL)

    def lay(step, source, row, still):
        def level(l, carry):
            for tracer, ext in enumerate((t_ext, s_ext)):
                for i in range(2):
                    ext[step, l, pl.ds(row + i, 1)] = source[tracer, pl.ds(i * levels + l, 1)]
            if step == 0:
                v_ext[l, pl.ds(still, 1)] = source[0, pl.ds(2 * levels + l, 1)]
                o_ext[l, pl.ds(still, 1)] = source[1, pl.ds(2 * levels + l, 1)]
            return carry

        lax.fori_loop(0, levels, level, 0, unroll=UNROLL)

    def crown():
        above_own = jnp.zeros((2, LANES), F32)

        def level(l, carry):
            for step in range(STEPS):
                t_ext[step, l, pl.ds(end, 2)] = above_own
                s_ext[step, l, pl.ds(end, 2)] = above_own
            v_ext[l, pl.ds(end, 2)] = above_own
            o_ext[l, pl.ds(end, 2)] = above_own
            under_top[0, pl.ds(l, 1)] = v_ext[l, pl.ds(end - 2, 1)]
            under_top[1, pl.ds(l, 1)] = o_ext[l, pl.ds(end - 2, 1)]
            under_top[2, pl.ds(l, 1)] = jnp.full((1, LANES), kappa_h[l], F32)
            return carry

        lax.fori_loop(0, levels, level, 0, unroll=UNROLL)

    def mend(step):
        first, second, still = pl.ds(0, levels), pl.ds(levels, levels), pl.ds(2 * levels, levels)
        every = pl.ds(0, levels)
        v2, o2, diffuse = under_top[0, every], under_top[1, every], under_top[2, every]
        v1, o1 = north[0, 0, still], north[0, 1, still]
        v_ghost, o_ghost = -over[0, 0, still], over[0, 1, still]
        lower = o2 * o1 * (v2 + v1) * (-1.0 / 24.0)
        speed, opened = v1 + v_ghost, o1 * o_ghost
        for tracer in range(2):
            c2, c1 = north[step, tracer, first], north[step, tracer, second]
            g1, g2 = over[step, tracer, second], over[step, tracer, first]
            missing = lower * g1
            face = flux(c1, g1, c2, g2, speed, opened, diffuse)
            mending[tracer, first] = o2 * missing
            mending[tracer, second] = o1 * (face - missing)

    def mend_rows(t_out, s_out, row):
        def level(l, carry):
            for tracer, out in enumerate((t_out, s_out)):
                for i in range(2):
                    here = pl.ds(row + i, 1)
                    out[l, here] = out[l, here] - mending[tracer, pl.ds(i * levels + l, 1)]
            return carry

        lax.fori_loop(0, levels, level, 0, unroll=UNROLL)

    def lay_south(step):
        under[...] = jnp.where(lat > 0, below[step], 0.0)
        lay(step, under, HALO - 2, HALO - 1)

    def lay_kappas():
        kappas[...] = lax.fori_loop(
            0,
            levels,
            lambda l, k: jnp.where((lane >= l * SLOT) & (lane < (l + 1) * SLOT), kappa_h[l], k),
            jnp.zeros((height, LANES), F32),
            unroll=UNROLL,
        )

    def make_faces(step):
        mine, theirs = cols[step], west[step]
        def at(x, p):
            return roll(x, (LANES - p) % LANES) if p else x

        for ref, back in ((face_t, 0), (face_s, 4)):
            speed = at(theirs, 8 - back) + at(mine, 9 - back)
            opened = at(theirs, 10 - back) * at(mine, 11 - back)
            ref[...] = flux(at(theirs, 1), at(mine, 2), theirs, at(mine, 3), speed, opened, kappas[...])

    def advance(step, t_out, s_out, shift):
        here, tall = own, height + 8
        theirs, other = west[step], east[step]
        faces = (face_t[...], face_s[...])

        def rise(k):
            return pl.ds(HALO - 1 + k, tall)

        def level(l, carry):
            base = l * SLOT
            diffuse = kappa_h[l]
            down, up = jnp.maximum(l - 1, 0), jnp.minimum(l + 1, levels - 1)
            k_down = jnp.where(l > 0, kappa_v[down], 0.0)
            k_up = jnp.where(l < levels - 1, kappa_v[jnp.minimum(l, levels - 2)], 0.0)
            u, o = u_own[l], o_ext[l, here]
            u_next = jnp.where(lane == LANES - 1, roll(other, 118 - base), roll(u, LANES - 1))
            o_next = jnp.where(lane == LANES - 1, roll(other, 116 - base), roll(o, LANES - 1))
            speed_x, open_x = u + u_next, o * o_next
            speed_y = v_ext[l, rise(0)] + v_ext[l, rise(1)]
            open_y = o_ext[l, rise(0)] * o_ext[l, rise(1)]
            lift = k_up * (o * o_ext[up, here])
            drop = k_down * (o * o_ext[down, here])
            for ext, out, face, back in ((t_ext, t_out, faces[0], 0), (s_ext, s_out, faces[1], 4)):
                c = ext[step, l, here]
                before = jnp.where(lane == 0, roll(theirs, 127 - back - base), roll(c, 1))
                next1 = jnp.where(lane == LANES - 1, roll(other, 125 - back - base), roll(c, LANES - 1))
                next2 = jnp.where(lane >= LANES - 2, roll(other, 124 - back - base), roll(c, LANES - 2))
                flux_x = flux(c, next1, before, next2, speed_x, open_x, diffuse)
                flux_w = jnp.where(lane == 0, roll(face, lax.rem(2 * LANES - back - base, LANES)), roll(flux_x, 1))
                flux_y = flux(
                    ext[step, l, rise(0)], ext[step, l, rise(1)], ext[step, l, rise(-1)], ext[step, l, rise(2)],
                    speed_y, open_y, diffuse,
                )
                flux_n = roll(flux_y, tall - 1, 0)
                gain = lift * (ext[step, up, here] - c) - drop * (c - ext[step, down, here])
                out[l, pl.ds(shift, height)] = c + o * (gain - (flux_x - flux_w) - (flux_n[:height] - flux_y[:height]))
            return carry

        lax.fori_loop(0, levels, level, 0, unroll=UNROLL)

    def wait_hop(step, tracer, near):
        for k in peers(near):
            hop(step, tracer, near, k).wait_recv()

    def picked(step, tracer, near):
        slots, at = (hop_near, near_slots) if near else (hop_far, far_slots)
        return slots[step][tracer][at[0]], slots[step][tracer][at[1]]

    def second_hop(step):
        for tracer, near in ((0, True), (1, False)):
            wait_hop(step, tracer, near)
            first, second = picked(step, tracer, near)
            first = jnp.take_along_axis(first, order, axis=1)
            second = jnp.take_along_axis(second, order, axis=1)
            relay[step, tracer] = jnp.where(near_part, first, second)
            for k in peers(not near):
                hop(step, tracer, not near, k).start()
            (hop_far if near else hop_near)[step][tracer][0] = relay[step, tracer]

    def choose(step):
        for tracer, near in ((0, False), (1, True)):
            wait_hop(step, tracer, near)
            first, second = picked(step, tracer, near)
            over[step, tracer] = jnp.where(near_part, first, second)

    for copy in first_rows:
        copy.wait()
    north[0, 1, pl.ds(2 * levels, levels)] = land_rows[0].astype(F32)
    south[0, 1, pl.ds(2 * levels, levels)] = land_rows[1].astype(F32)

    @pl.when(top)
    def _():
        pl.semaphore_wait(barrier, expected)
        first_hop(0)

    for load in loads:
        load.wait()

    def ocean(l, carry):
        o_ext[l, own] = land_own[l].astype(F32)
        return carry

    lax.fori_loop(0, levels, ocean, 0, unroll=UNROLL)
    pack_cols(0)
    lay_kappas()

    @pl.when(top)
    def _():
        crown()

    @pl.when(jnp.logical_not(top))
    def _():
        pl.semaphore_wait(barrier, expected)

    @pl.when(lat < nlat - 1)
    def _():
        to_north(0).start()

    @pl.when(lat > 0)
    def _():
        to_south(0).start()

    shift = (partner[0] + lon * LANES) & (nlon * LANES - 1)
    tile, offset = shift // LANES, shift & (LANES - 1)
    tile_far, tile_place = tile // WIDE, lax.rem(tile, WIDE)
    edge_lane = lax.broadcasted_iota(jnp.int32, (EDGE, LANES), 1)
    order = (offset - edge_lane) & (LANES - 1)
    near_part = edge_lane <= offset
    borrow0 = jnp.where(tile_place < place, 1, 0)
    borrow1 = jnp.where(tile_place - 1 < place, 1, 0)

    near_slots = [lax.rem(2 * place - tile_place + i + WIDE, WIDE) for i in range(2)]
    far_slots = [lax.rem(2 * far - tile_far + borrow + 2 * groups, groups) for borrow in (borrow0, borrow1)]

    for step in range(STEPS):
        last = step == STEPS - 1
        t_out, s_out, at = (temp_out, salt_out, 0) if last else (t_ext.at[step + 1], s_ext.at[step + 1], HALO)
        if step:
            pack_cols(step)
        to_right(step).start()
        to_left(step).start()

        @pl.when(top)
        def _():
            second_hop(step)

        @pl.when(lat > 0)
        def _():
            to_north(step).wait_recv()

        lay_south(step)

        @pl.when(lat < nlat - 1)
        def _():
            to_south(step).wait_recv()
            lay(step, above.at[step], end, end)

        to_right(step).wait_recv()
        to_left(step).wait_recv()
        make_faces(step)
        advance(step, t_out, s_out, at)
        if not last:
            pack_rows(step + 1, south, HALO)

            @pl.when(lat > 0)
            def _():
                to_south(step + 1).start()

            pack_rows(step + 1, north, end - 2)

            @pl.when(lat < nlat - 1)
            def _():
                to_north(step + 1).start()

        @pl.when(top)
        def _():
            choose(step)
            mend(step)
            if not last:
                both = pl.ds(0, 2 * levels)
                for tracer in range(2):
                    north[step + 1, tracer, both] = north[step + 1, tracer, both] - mending[tracer, both]
                first_hop(step + 1)
            mend_rows(t_out, s_out, at + height - 2)

    for step in range(STEPS):
        to_right(step).wait_send()
        to_left(step).wait_send()

        @pl.when(lat < nlat - 1)
        def _():
            to_north(step).wait_send()

        @pl.when(lat > 0)
        def _():
            to_south(step).wait_send()

        @pl.when(top)
        def _():
            for tracer in range(2):
                for near in (True, False):
                    for k in peers(near):
                        hop(step, tracer, near, k).wait_send()


def hand_over(temp, salt, temp_out, salt_out):
    temp_out[...] = temp[...]
    salt_out[...] = salt[...]


def local(nlon, nlat, temp, salt, u_vel, v_vel, land_sea, partner, kappa_h, kappa_v):
    levels, height, width = temp.shape
    block = jax.ShapeDtypeStruct(temp.shape, F32)
    anywhere = pl.BlockSpec(memory_space=pl.ANY)
    groups = nlon // WIDE

    def room(*shape):
        return pltpu.VMEM(shape, F32)

    tall = height + 24
    results = pl.pallas_call(
        functools.partial(kernel, nlon, nlat),
        out_shape=(block, block),
        in_specs=[anywhere] * 8,
        out_specs=[pl.BlockSpec(memory_space=pltpu.VMEM)] * 2,
        scratch_shapes=[
            pltpu.SMEM(partner.shape, jnp.int32),
            pltpu.SMEM(kappa_h.shape, F32),
            pltpu.SMEM(kappa_v.shape, F32),
            room(STEPS, levels, tall, width),
            room(STEPS, levels, tall, width),
            room(levels, tall, width),
            room(levels, tall, width),
            room(levels, height, width),
            pltpu.VMEM((levels, height, width), jnp.int32),
            pltpu.VMEM((2, levels, width), jnp.int32),
            room(STEPS, height, width),
            room(STEPS, 2, EDGE, width),
            room(STEPS, 2, EDGE, width),
            room(STEPS, 2, EDGE, width),
            room(STEPS, height, width),
            room(STEPS, height, width),
            room(STEPS, 2, EDGE, width),
            room(STEPS, 2, EDGE, width),
            *[room(WIDE, EDGE, width)] * (2 * STEPS),
            *[room(groups, EDGE, width)] * (2 * STEPS),
            room(2, EDGE, width),
            room(STEPS, 2, EDGE, width),
            room(3, 16, width),
            room(2, EDGE, width),
            room(height, width),
            room(height, width),
            room(height, width),
            pltpu.SemaphoreType.DMA((8,)),
            pltpu.SemaphoreType.DMA((12,)),
            pltpu.SemaphoreType.DMA((STEPS, 4)),
            pltpu.SemaphoreType.DMA((STEPS, 4)),
            pltpu.SemaphoreType.DMA((STEPS, 2, WIDE)),
            pltpu.SemaphoreType.DMA((STEPS, 2, WIDE)),
            pltpu.SemaphoreType.DMA((STEPS, 2, groups)),
            pltpu.SemaphoreType.DMA((STEPS, 2, groups)),
        ],
        compiler_params=pltpu.CompilerParams(collective_id=0, has_side_effects=True, vmem_limit_bytes=60 << 20),
        name="tracer_steps",
    )(temp, salt, u_vel, v_vel, land_sea, partner, kappa_h, kappa_v)
    return pl.pallas_call(
        hand_over,
        out_shape=(block, block),
        grid=(2,),
        in_specs=[pl.BlockSpec((levels // 2, height, width), lambda i: (i, 0, 0))] * 2,
        out_specs=[pl.BlockSpec((levels // 2, height, width), lambda i: (i, 0, 0))] * 2,
        compiler_params=pltpu.CompilerParams(vmem_limit_bytes=60 << 20),
        name="hand_over",
    )(*results)


def solution(mesh):
    field = P(None, "lat", "lon")
    return jax.shard_map(
        functools.partial(local, mesh.shape["lon"], mesh.shape["lat"]),
        mesh=mesh,
        in_specs=(field,) * 5 + (P("lon"), P(), P()),
        out_specs=(field, field),
        check_vma=False,
    )
```

```python
import functools

import jax
import jax.numpy as jnp
from jax import lax
from jax.experimental import pallas as pl
from jax.experimental.pallas import tpu as pltpu
from jax.sharding import PartitionSpec as P

STEPS = 2
WIDE = 8
LANES = 128
SLOT = 12
EDGE = 32
UNROLL = 5
F32 = jnp.float32
MESH = pl.DeviceIdType.MESH
HALO = 8


def roll(x, shift, axis=1):
    return pltpu.roll(x, shift, axis)


def flux(c0, c1, before, after, speed, opened, diffuse):
    return opened * (speed * ((7.0 * (c0 + c1) - (before + after)) * (1.0 / 24.0)) - diffuse * (c1 - c0))


def kernel(
    nlon, nlat, temp, salt, u_vel, v_vel, land, partner_in, kappas_in, temp_out, salt_out,
    partner, coefficients,
    t_ext, s_ext, v_ext, o_ext, u_own, land_own, land_rows, cols, north, south, relay, west, east, below, above,
    near00, near01, near10, near11, far00, far01, far10, far11, under, over, under_top, mending,
    face_t, face_s, kappas,
    load_sem, row_sem, send, recv, near_send, near_recv, far_send, far_recv,
):
    hop_near, hop_far = ((near00, near01), (near10, near11)), ((far00, far01), (far10, far11))
    levels, height, _ = temp.shape
    end = HALO + height
    lon, lat = lax.axis_index("lon"), lax.axis_index("lat")
    top = lat == nlat - 1
    right, left = lax.rem(lon + 1, nlon), lax.rem(lon + nlon - 1, nlon)
    place, far = lax.rem(lon, WIDE), lon // WIDE
    groups = nlon // WIDE

    def farthest_first(count):
        return sorted(range(1, count), key=lambda k: -min(k, count - k))

    def in_group(k):
        return far * WIDE + lax.rem(place + k, WIDE)

    def in_across(k):
        return lax.rem(far + k, groups) * WIDE + place

    def row_copy(field, row, dst, i):
        return pltpu.make_async_copy(field.at[:, row], dst, row_sem.at[i])

    first_rows = [
        row_copy(temp, height - 2, north.at[0, 0, pl.ds(0, levels)], 0),
        row_copy(temp, height - 1, north.at[0, 0, pl.ds(levels, levels)], 1),
        row_copy(v_vel, height - 1, north.at[0, 0, pl.ds(2 * levels, levels)], 2),
        row_copy(salt, height - 2, north.at[0, 1, pl.ds(0, levels)], 3),
        row_copy(salt, height - 1, north.at[0, 1, pl.ds(levels, levels)], 4),
        row_copy(land, height - 1, land_rows.at[0], 5),
        row_copy(temp, 0, south.at[0, 0, pl.ds(0, levels)], 6),
        row_copy(temp, 1, south.at[0, 0, pl.ds(levels, levels)], 7),
        row_copy(v_vel, 0, south.at[0, 0, pl.ds(2 * levels, levels)], 8),
        row_copy(salt, 0, south.at[0, 1, pl.ds(0, levels)], 9),
        row_copy(salt, 1, south.at[0, 1, pl.ds(levels, levels)], 10),
        row_copy(land, 0, land_rows.at[1], 11),
    ]
    loads = [
        pltpu.make_async_copy(src, dst, load_sem.at[i])
        for i, (src, dst) in enumerate(
            (
                (temp, t_ext.at[0, :, pl.ds(HALO, height)]),
                (salt, s_ext.at[0, :, pl.ds(HALO, height)]),
                (v_vel, v_ext.at[:, pl.ds(HALO, height)]),
                (land, land_own),
                (u_vel, u_own),
                (partner_in, partner),
                (kappas_in, coefficients),
            )
        )
    ]
    for copy in first_rows[:6]:
        copy.start()

    barrier = pltpu.get_barrier_semaphore()

    def greet(a, b):
        pl.semaphore_signal(barrier, inc=1, device_id=(a, b), device_id_type=MESH)

    @pl.when(top)
    def _():
        for k in range(1, WIDE):
            greet(in_group(k), lat)
        for k in range(1, groups):
            greet(in_across(k), lat)

    greet(right, lat)
    greet(left, lat)

    @pl.when(lat > 0)
    def _():
        greet(lon, lat - 1)

    @pl.when(lat < nlat - 1)
    def _():
        greet(lon, lat + 1)

    expected = 2 + jnp.where(lat > 0, 1, 0) + jnp.where(top, WIDE + groups - 2, 1)

    for copy in first_rows[6:] + loads:
        copy.start()

    def remote(src, dst, sent, got, a, b):
        return pltpu.make_async_remote_copy(
            src_ref=src, dst_ref=dst, send_sem=sent, recv_sem=got, device_id=(a, b), device_id_type=MESH
        )

    def rows(step):
        return pl.ds(0, (3 if step == 0 else 2) * levels)

    def to_right(step):
        return remote(cols.at[step], west.at[step], send.at[step, 0], recv.at[step, 0], right, lat)

    def to_left(step):
        return remote(cols.at[step], east.at[step], send.at[step, 1], recv.at[step, 1], left, lat)

    def to_north(step):
        return remote(
            north.at[step, :, rows(step)], below.at[step, :, rows(step)], send.at[step, 2], recv.at[step, 2],
            lon, lax.rem(lat + 1, nlat),
        )

    def to_south(step):
        return remote(
            south.at[step, :, rows(step)], above.at[step, :, rows(step)], send.at[step, 3], recv.at[step, 3],
            lon, lax.rem(lat + nlat - 1, nlat),
        )

    def hop(step, tracer, near, k):
        message = (north if near == (tracer == 0) else relay).at[step, tracer, rows(step)]
        slots, sent, got, to = (
            (hop_near, near_send, near_recv, in_group) if near else (hop_far, far_send, far_recv, in_across)
        )
        return remote(
            message, slots[step][tracer].at[k, rows(step)], sent.at[step, tracer, k], got.at[step, tracer, k], to(k), lat
        )

    def peers(near):
        return farthest_first(WIDE if near else groups)

    def first_hop(step):
        for k in range(max(WIDE, groups)):
            for tracer, near in ((0, True), (1, False)):
                if k < len(peers(near)):
                    hop(step, tracer, near, peers(near)[k]).start()
        hop_near[step][0][0] = north[step, 0]
        hop_far[step][1][0] = north[step, 1]

    def pack_rows(step, ref, row):
        def level(l, carry):
            for tracer, ext in enumerate((t_ext, s_ext)):
                for i in range(2):
                    ref[step, tracer, pl.ds(i * levels + l, 1)] = ext[step, l, pl.ds(row + i, 1)]
            return carry

        lax.fori_loop(0, levels, level, 0, unroll=UNROLL)

    lane = lax.broadcasted_iota(jnp.int32, (height, LANES), 1)
    own = pl.ds(HALO, height)

    def pack_cols(step):
        def level(l, held):
            base = l * SLOT
            here = lane - base
            held = jnp.where((here >= 0) & (here < 4), roll(t_ext[step, l, own], base + 2), held)
            held = jnp.where((here >= 4) & (here < 8), roll(s_ext[step, l, own], base + 6), held)
            if step == 0:
                held = jnp.where((here >= 8) & (here < 10), roll(u_own[l], base + 9), held)
                held = jnp.where((here >= 10) & (here < 12), roll(o_ext[l, own], base + 11), held)
            return held

        cols[step] = lax.fori_loop(0, levels, level, cols[0] if step else jnp.zeros((height, LANES), F32), unroll=UNROLL)

    def lay(step, source, row, still):
        def level(l, carry):
            for tracer, ext in enumerate((t_ext, s_ext)):
                for i in range(2):
                    ext[step, l, pl.ds(row + i, 1)] = source[tracer, pl.ds(i * levels + l, 1)]
            if step == 0:
                v_ext[l, pl.ds(still, 1)] = source[0, pl.ds(2 * levels + l, 1)]
                o_ext[l, pl.ds(still, 1)] = source[1, pl.ds(2 * levels + l, 1)]
            return carry

        lax.fori_loop(0, levels, level, 0, unroll=UNROLL)

    def crown():
        above_own = jnp.zeros((2, LANES), F32)

        def level(l, carry):
            for step in range(STEPS):
                t_ext[step, l, pl.ds(end, 2)] = above_own
                s_ext[step, l, pl.ds(end, 2)] = above_own
            v_ext[l, pl.ds(end, 2)] = above_own
            o_ext[l, pl.ds(end, 2)] = above_own
            under_top[0, pl.ds(l, 1)] = v_ext[l, pl.ds(end - 2, 1)]
            under_top[1, pl.ds(l, 1)] = o_ext[l, pl.ds(end - 2, 1)]
            under_top[2, pl.ds(l, 1)] = jnp.full((1, LANES), coefficients[l], F32)
            return carry

        lax.fori_loop(0, levels, level, 0, unroll=UNROLL)

    def mend(step):
        first, second, still = pl.ds(0, levels), pl.ds(levels, levels), pl.ds(2 * levels, levels)
        every = pl.ds(0, levels)
        v2, o2, diffuse = under_top[0, every], under_top[1, every], under_top[2, every]
        v1, o1 = north[0, 0, still], north[0, 1, still]
        v_ghost, o_ghost = -over[0, 0, still], over[0, 1, still]
        lower = o2 * o1 * (v2 + v1) * (-1.0 / 24.0)
        speed, opened = v1 + v_ghost, o1 * o_ghost
        for tracer in range(2):
            c2, c1 = north[step, tracer, first], north[step, tracer, second]
            g1, g2 = over[step, tracer, second], over[step, tracer, first]
            missing = lower * g1
            face = flux(c1, g1, c2, g2, speed, opened, diffuse)
            mending[tracer, first] = o2 * missing
            mending[tracer, second] = o1 * (face - missing)

    def mend_rows(t_out, s_out, row):
        def level(l, carry):
            for tracer, out in enumerate((t_out, s_out)):
                for i in range(2):
                    here = pl.ds(row + i, 1)
                    out[l, here] = out[l, here] - mending[tracer, pl.ds(i * levels + l, 1)]
            return carry

        lax.fori_loop(0, levels, level, 0, unroll=UNROLL)

    def lay_south(step):
        under[...] = jnp.where(lat > 0, below[step], 0.0)
        lay(step, under, HALO - 2, HALO - 1)

    def lay_kappas():
        kappas[...] = lax.fori_loop(
            0,
            levels,
            lambda l, k: jnp.where((lane >= l * SLOT) & (lane < (l + 1) * SLOT), coefficients[l], k),
            jnp.zeros((height, LANES), F32),
            unroll=UNROLL,
        )

    def make_faces(step):
        mine, theirs = cols[step], west[step]
        def at(x, p):
            return roll(x, (LANES - p) % LANES) if p else x

        for ref, back in ((face_t, 0), (face_s, 4)):
            speed = at(theirs, 8 - back) + at(mine, 9 - back)
            opened = at(theirs, 10 - back) * at(mine, 11 - back)
            ref[...] = flux(at(theirs, 1), at(mine, 2), theirs, at(mine, 3), speed, opened, kappas[...])

    def advance(step, t_out, s_out, shift):
        here, tall = own, height + 8
        theirs, other = west[step], east[step]
        faces = (face_t[...], face_s[...])

        def rise(k):
            return pl.ds(HALO - 1 + k, tall)

        def level(l, carry):
            base = l * SLOT
            diffuse = coefficients[l]
            down, up = jnp.maximum(l - 1, 0), jnp.minimum(l + 1, levels - 1)
            k_down = jnp.where(l > 0, coefficients[levels + down], 0.0)
            k_up = jnp.where(l < levels - 1, coefficients[levels + jnp.minimum(l, levels - 2)], 0.0)
            u, o = u_own[l], o_ext[l, here]
            u_next = jnp.where(lane == LANES - 1, roll(other, 118 - base), roll(u, LANES - 1))
            o_next = jnp.where(lane == LANES - 1, roll(other, 116 - base), roll(o, LANES - 1))
            speed_x, open_x = u + u_next, o * o_next
            speed_y = v_ext[l, rise(0)] + v_ext[l, rise(1)]
            open_y = o_ext[l, rise(0)] * o_ext[l, rise(1)]
            lift = k_up * (o * o_ext[up, here])
            drop = k_down * (o * o_ext[down, here])
            for ext, out, face, back in ((t_ext, t_out, faces[0], 0), (s_ext, s_out, faces[1], 4)):
                c = ext[step, l, here]
                before = jnp.where(lane == 0, roll(theirs, 127 - back - base), roll(c, 1))
                next1 = jnp.where(lane == LANES - 1, roll(other, 125 - back - base), roll(c, LANES - 1))
                next2 = jnp.where(lane >= LANES - 2, roll(other, 124 - back - base), roll(c, LANES - 2))
                flux_x = flux(c, next1, before, next2, speed_x, open_x, diffuse)
                flux_w = jnp.where(lane == 0, roll(face, lax.rem(2 * LANES - back - base, LANES)), roll(flux_x, 1))
                flux_y = flux(
                    ext[step, l, rise(0)], ext[step, l, rise(1)], ext[step, l, rise(-1)], ext[step, l, rise(2)],
                    speed_y, open_y, diffuse,
                )
                flux_n = roll(flux_y, tall - 1, 0)
                gain = lift * (ext[step, up, here] - c) - drop * (c - ext[step, down, here])
                out[l, pl.ds(shift, height)] = c + o * (gain - (flux_x - flux_w) - (flux_n[:height] - flux_y[:height]))
            return carry

        lax.fori_loop(0, levels, level, 0, unroll=UNROLL)

    def wait_hop(step, tracer, near):
        for k in peers(near):
            hop(step, tracer, near, k).wait_recv()

    def picked(step, tracer, near):
        slots, at = (hop_near, near_slots) if near else (hop_far, far_slots)
        return slots[step][tracer][at[0]], slots[step][tracer][at[1]]

    def second_hop(step):
        for tracer, near in ((0, True), (1, False)):
            wait_hop(step, tracer, near)
            first, second = picked(step, tracer, near)
            first = jnp.take_along_axis(first, order, axis=1)
            second = jnp.take_along_axis(second, order, axis=1)
            relay[step, tracer] = jnp.where(near_part, first, second)
            for k in peers(not near):
                hop(step, tracer, not near, k).start()
            (hop_far if near else hop_near)[step][tracer][0] = relay[step, tracer]

    def choose(step):
        for tracer, near in ((0, False), (1, True)):
            wait_hop(step, tracer, near)
            first, second = picked(step, tracer, near)
            over[step, tracer] = jnp.where(near_part, first, second)

    for copy in first_rows[:6]:
        copy.wait()
    north[0, 1, pl.ds(2 * levels, levels)] = land_rows[0].astype(F32)

    @pl.when(top)
    def _():
        pl.semaphore_wait(barrier, expected)
        first_hop(0)

    for copy in first_rows[6:]:
        copy.wait()
    south[0, 1, pl.ds(2 * levels, levels)] = land_rows[1].astype(F32)
    for load in loads:
        load.wait()

    def ocean(l, carry):
        o_ext[l, own] = land_own[l].astype(F32)
        return carry

    lax.fori_loop(0, levels, ocean, 0, unroll=UNROLL)
    pack_cols(0)
    lay_kappas()

    @pl.when(top)
    def _():
        crown()

    @pl.when(jnp.logical_not(top))
    def _():
        pl.semaphore_wait(barrier, expected)

    @pl.when(lat < nlat - 1)
    def _():
        to_north(0).start()

    @pl.when(lat > 0)
    def _():
        to_south(0).start()

    shift = (partner[0] + lon * LANES) & (nlon * LANES - 1)
    tile, offset = shift // LANES, shift & (LANES - 1)
    tile_far, tile_place = tile // WIDE, lax.rem(tile, WIDE)
    edge_lane = lax.broadcasted_iota(jnp.int32, (EDGE, LANES), 1)
    order = (offset - edge_lane) & (LANES - 1)
    near_part = edge_lane <= offset
    borrow0 = jnp.where(tile_place < place, 1, 0)
    borrow1 = jnp.where(tile_place - 1 < place, 1, 0)

    near_slots = [lax.rem(2 * place - tile_place + i + WIDE, WIDE) for i in range(2)]
    far_slots = [lax.rem(2 * far - tile_far + borrow + 2 * groups, groups) for borrow in (borrow0, borrow1)]

    for step in range(STEPS):
        last = step == STEPS - 1
        t_out, s_out, at = (temp_out, salt_out, 0) if last else (t_ext.at[step + 1], s_ext.at[step + 1], HALO)
        if step:
            pack_cols(step)
        to_right(step).start()
        to_left(step).start()

        @pl.when(top)
        def _():
            second_hop(step)

        @pl.when(lat > 0)
        def _():
            to_north(step).wait_recv()

        lay_south(step)

        @pl.when(lat < nlat - 1)
        def _():
            to_south(step).wait_recv()
            lay(step, above.at[step], end, end)

        to_right(step).wait_recv()
        to_left(step).wait_recv()
        make_faces(step)
        advance(step, t_out, s_out, at)
        if not last:
            pack_rows(step + 1, south, HALO)

            @pl.when(lat > 0)
            def _():
                to_south(step + 1).start()

            pack_rows(step + 1, north, end - 2)

            @pl.when(lat < nlat - 1)
            def _():
                to_north(step + 1).start()

        @pl.when(top)
        def _():
            choose(step)
            mend(step)
            if not last:
                both = pl.ds(0, 2 * levels)
                for tracer in range(2):
                    north[step + 1, tracer, both] = north[step + 1, tracer, both] - mending[tracer, both]
                first_hop(step + 1)
            mend_rows(t_out, s_out, at + height - 2)

    for step in range(STEPS):
        to_right(step).wait_send()
        to_left(step).wait_send()

        @pl.when(lat < nlat - 1)
        def _():
            to_north(step).wait_send()

        @pl.when(lat > 0)
        def _():
            to_south(step).wait_send()

        @pl.when(top)
        def _():
            for tracer in range(2):
                for near in (True, False):
                    for k in peers(near):
                        hop(step, tracer, near, k).wait_send()


def hand_over(temp, salt, temp_out, salt_out, sem):
    copies = [pltpu.make_async_copy(a, b, sem.at[i]) for i, (a, b) in enumerate(((temp, temp_out), (salt, salt_out)))]
    for copy in copies:
        copy.start()
    for copy in copies:
        copy.wait()


def local(nlon, nlat, temp, salt, u_vel, v_vel, land_sea, partner, kappa_h, kappa_v):
    levels, height, width = temp.shape
    block = jax.ShapeDtypeStruct(temp.shape, F32)
    anywhere = pl.BlockSpec(memory_space=pl.ANY)
    groups = nlon // WIDE

    def room(*shape):
        return pltpu.VMEM(shape, F32)

    tall = height + 24
    results = pl.pallas_call(
        functools.partial(kernel, nlon, nlat),
        out_shape=(block, block),
        in_specs=[anywhere] * 7,
        out_specs=[pl.BlockSpec(memory_space=pltpu.VMEM)] * 2,
        scratch_shapes=[
            pltpu.SMEM(partner.shape, jnp.int32),
            pltpu.SMEM((2 * levels - 1,), F32),
            room(STEPS, levels, tall, width),
            room(STEPS, levels, tall, width),
            room(levels, tall, width),
            room(levels, tall, width),
            room(levels, height, width),
            pltpu.VMEM((levels, height, width), jnp.int32),
            pltpu.VMEM((2, levels, width), jnp.int32),
            room(STEPS, height, width),
            room(STEPS, 2, EDGE, width),
            room(STEPS, 2, EDGE, width),
            room(STEPS, 2, EDGE, width),
            room(STEPS, height, width),
            room(STEPS, height, width),
            room(STEPS, 2, EDGE, width),
            room(STEPS, 2, EDGE, width),
            *[room(WIDE, EDGE, width)] * (2 * STEPS),
            *[room(groups, EDGE, width)] * (2 * STEPS),
            room(2, EDGE, width),
            room(STEPS, 2, EDGE, width),
            room(3, 16, width),
            room(2, EDGE, width),
            room(height, width),
            room(height, width),
            room(height, width),
            pltpu.SemaphoreType.DMA((7,)),
            pltpu.SemaphoreType.DMA((12,)),
            pltpu.SemaphoreType.DMA((STEPS, 4)),
            pltpu.SemaphoreType.DMA((STEPS, 4)),
            pltpu.SemaphoreType.DMA((STEPS, 2, WIDE)),
            pltpu.SemaphoreType.DMA((STEPS, 2, WIDE)),
            pltpu.SemaphoreType.DMA((STEPS, 2, groups)),
            pltpu.SemaphoreType.DMA((STEPS, 2, groups)),
        ],
        compiler_params=pltpu.CompilerParams(collective_id=0, has_side_effects=True, vmem_limit_bytes=54880 << 10),
        name="tracer_steps",
    )(temp, salt, u_vel, v_vel, land_sea, partner, jnp.concatenate([kappa_h, kappa_v]))
    return results


def solution(mesh):
    field = P(None, "lat", "lon")
    return jax.shard_map(
        functools.partial(local, mesh.shape["lon"], mesh.shape["lat"]),
        mesh=mesh,
        in_specs=(field,) * 5 + (P("lon"), P(), P()),
        out_specs=(field, field),
        check_vma=False,
    )
```

```python
import functools

import jax
import jax.numpy as jnp
from jax import lax
from jax.experimental import pallas as pl
from jax.experimental.pallas import tpu as pltpu
from jax.sharding import PartitionSpec as P

STEPS = 2
WIDE = 8
LANES = 128
SLOT = 12
EDGE = 32
UNROLL = 5
F32 = jnp.float32
MESH = pl.DeviceIdType.MESH
HALO = 8


def roll(x, shift, axis=1):
    return pltpu.roll(x, shift, axis)


def flux(c0, c1, before, after, speed, opened, diffuse):
    return opened * (speed * ((7.0 * (c0 + c1) - (before + after)) * (1.0 / 24.0)) - diffuse * (c1 - c0))


def kernel(
    nlon, nlat, temp, salt, u_vel, v_vel, land, partner_in, kappas_in, temp_out, salt_out,
    partner, coefficients,
    t_ext, s_ext, v_ext, o_ext, u_own, land_own, land_rows, cols, north, south, relay, west, east, below, above,
    near00, near01, near10, near11, far00, far01, far10, far11, under, over, under_top, mending,
    face_t, face_s, kappas,
    load_sem, row_sem, send, recv, near_send, near_recv, far_send, far_recv,
):
    hop_near, hop_far = ((near00, near01), (near10, near11)), ((far00, far01), (far10, far11))
    levels, height, _ = temp.shape
    end = HALO + height
    lon, lat = lax.axis_index("lon"), lax.axis_index("lat")
    top = lat == nlat - 1
    right, left = lax.rem(lon + 1, nlon), lax.rem(lon + nlon - 1, nlon)
    place, far = lax.rem(lon, WIDE), lon // WIDE
    groups = nlon // WIDE

    def farthest_first(count):
        return sorted(range(1, count), key=lambda k: -min(k, count - k))

    def in_group(k):
        return far * WIDE + lax.rem(place + k, WIDE)

    def in_across(k):
        return lax.rem(far + k, groups) * WIDE + place

    def row_copy(field, row, dst, i):
        return pltpu.make_async_copy(field.at[:, row], dst, row_sem.at[i])

    first_rows = [
        row_copy(temp, height - 2, north.at[0, 0, pl.ds(0, levels)], 0),
        row_copy(temp, height - 1, north.at[0, 0, pl.ds(levels, levels)], 1),
        row_copy(v_vel, height - 1, north.at[0, 0, pl.ds(2 * levels, levels)], 2),
        row_copy(salt, height - 2, north.at[0, 1, pl.ds(0, levels)], 3),
        row_copy(salt, height - 1, north.at[0, 1, pl.ds(levels, levels)], 4),
        row_copy(land, height - 1, land_rows.at[0], 5),
        row_copy(temp, 0, south.at[0, 0, pl.ds(0, levels)], 6),
        row_copy(temp, 1, south.at[0, 0, pl.ds(levels, levels)], 7),
        row_copy(v_vel, 0, south.at[0, 0, pl.ds(2 * levels, levels)], 8),
        row_copy(salt, 0, south.at[0, 1, pl.ds(0, levels)], 9),
        row_copy(salt, 1, south.at[0, 1, pl.ds(levels, levels)], 10),
        row_copy(land, 0, land_rows.at[1], 11),
    ]
    loads = [
        pltpu.make_async_copy(src, dst, load_sem.at[i])
        for i, (src, dst) in enumerate(
            (
                (temp, t_ext.at[0, :, pl.ds(HALO, height)]),
                (salt, s_ext.at[0, :, pl.ds(HALO, height)]),
                (v_vel, v_ext.at[:, pl.ds(HALO, height)]),
                (land, land_own),
                (u_vel, u_own),
                (partner_in, partner),
                (kappas_in, coefficients),
            )
        )
    ]
    barrier = pltpu.get_barrier_semaphore()

    def greet(a, b):
        pl.semaphore_signal(barrier, inc=1, device_id=(a, b), device_id_type=MESH)

    @pl.when(top)
    def _():
        for k in farthest_first(groups):
            greet(in_across(k), lat)
        for k in farthest_first(WIDE):
            greet(in_group(k), lat)

    greet(right, lat)
    greet(left, lat)

    @pl.when(lat > 0)
    def _():
        greet(lon, lat - 1)

    @pl.when(lat < nlat - 1)
    def _():
        greet(lon, lat + 1)

    expected = 2 + jnp.where(lat > 0, 1, 0) + jnp.where(top, WIDE + groups - 2, 1)

    for copy in first_rows + loads:
        copy.start()

    def remote(src, dst, sent, got, a, b):
        return pltpu.make_async_remote_copy(
            src_ref=src, dst_ref=dst, send_sem=sent, recv_sem=got, device_id=(a, b), device_id_type=MESH
        )

    def rows(step):
        return pl.ds(0, (3 if step == 0 else 2) * levels)

    def to_right(step):
        return remote(cols.at[step], west.at[step], send.at[step, 0], recv.at[step, 0], right, lat)

    def to_left(step):
        return remote(cols.at[step], east.at[step], send.at[step, 1], recv.at[step, 1], left, lat)

    def to_north(step):
        return remote(
            north.at[step, :, rows(step)], below.at[step, :, rows(step)], send.at[step, 2], recv.at[step, 2],
            lon, lax.rem(lat + 1, nlat),
        )

    def to_south(step):
        return remote(
            south.at[step, :, rows(step)], above.at[step, :, rows(step)], send.at[step, 3], recv.at[step, 3],
            lon, lax.rem(lat + nlat - 1, nlat),
        )

    def hop(step, tracer, near, k):
        message = (north if near == (tracer == 0) else relay).at[step, tracer, rows(step)]
        slots, sent, got, to = (
            (hop_near, near_send, near_recv, in_group) if near else (hop_far, far_send, far_recv, in_across)
        )
        return remote(
            message, slots[step][tracer].at[k, rows(step)], sent.at[step, tracer, k], got.at[step, tracer, k], to(k), lat
        )

    def peers(near):
        return farthest_first(WIDE if near else groups)

    def first_hop(step):
        for k in range(max(WIDE, groups)):
            for tracer, near in ((0, True), (1, False)):
                if k < len(peers(near)):
                    hop(step, tracer, near, peers(near)[k]).start()
        hop_near[step][0][0] = north[step, 0]
        hop_far[step][1][0] = north[step, 1]

    def pack_rows(step, ref, row):
        def level(l, carry):
            for tracer, ext in enumerate((t_ext, s_ext)):
                for i in range(2):
                    ref[step, tracer, pl.ds(i * levels + l, 1)] = ext[step, l, pl.ds(row + i, 1)]
            return carry

        lax.fori_loop(0, levels, level, 0, unroll=UNROLL)

    lane = lax.broadcasted_iota(jnp.int32, (height, LANES), 1)
    own = pl.ds(HALO, height)

    def pack_cols(step):
        def level(l, held):
            base = l * SLOT
            here = lane - base
            held = jnp.where((here >= 0) & (here < 4), roll(t_ext[step, l, own], base + 2), held)
            held = jnp.where((here >= 4) & (here < 8), roll(s_ext[step, l, own], base + 6), held)
            if step == 0:
                held = jnp.where((here >= 8) & (here < 10), roll(u_own[l], base + 9), held)
                held = jnp.where((here >= 10) & (here < 12), roll(o_ext[l, own], base + 11), held)
            return held

        cols[step] = lax.fori_loop(0, levels, level, cols[0] if step else jnp.zeros((height, LANES), F32), unroll=UNROLL)

    def lay(step, source, row, still):
        def level(l, carry):
            for tracer, ext in enumerate((t_ext, s_ext)):
                for i in range(2):
                    ext[step, l, pl.ds(row + i, 1)] = source[tracer, pl.ds(i * levels + l, 1)]
            if step == 0:
                v_ext[l, pl.ds(still, 1)] = source[0, pl.ds(2 * levels + l, 1)]
                o_ext[l, pl.ds(still, 1)] = source[1, pl.ds(2 * levels + l, 1)]
            return carry

        lax.fori_loop(0, levels, level, 0, unroll=UNROLL)

    def crown():
        above_own = jnp.zeros((2, LANES), F32)

        def level(l, carry):
            for step in range(STEPS):
                t_ext[step, l, pl.ds(end, 2)] = above_own
                s_ext[step, l, pl.ds(end, 2)] = above_own
            v_ext[l, pl.ds(end, 2)] = above_own
            o_ext[l, pl.ds(end, 2)] = above_own
            under_top[0, pl.ds(l, 1)] = v_ext[l, pl.ds(end - 2, 1)]
            under_top[1, pl.ds(l, 1)] = o_ext[l, pl.ds(end - 2, 1)]
            under_top[2, pl.ds(l, 1)] = jnp.full((1, LANES), coefficients[l], F32)
            return carry

        lax.fori_loop(0, levels, level, 0, unroll=UNROLL)

    def mend(step):
        first, second, still = pl.ds(0, levels), pl.ds(levels, levels), pl.ds(2 * levels, levels)
        every = pl.ds(0, levels)
        v2, o2, diffuse = under_top[0, every], under_top[1, every], under_top[2, every]
        v1, o1 = north[0, 0, still], north[0, 1, still]
        v_ghost, o_ghost = -over[0, 0, still], over[0, 1, still]
        lower = o2 * o1 * (v2 + v1) * (-1.0 / 24.0)
        speed, opened = v1 + v_ghost, o1 * o_ghost
        for tracer in range(2):
            c2, c1 = north[step, tracer, first], north[step, tracer, second]
            g1, g2 = over[step, tracer, second], over[step, tracer, first]
            missing = lower * g1
            face = flux(c1, g1, c2, g2, speed, opened, diffuse)
            mending[tracer, first] = o2 * missing
            mending[tracer, second] = o1 * (face - missing)

    def mend_rows(t_out, s_out, row):
        def level(l, carry):
            for tracer, out in enumerate((t_out, s_out)):
                for i in range(2):
                    here = pl.ds(row + i, 1)
                    out[l, here] = out[l, here] - mending[tracer, pl.ds(i * levels + l, 1)]
            return carry

        lax.fori_loop(0, levels, level, 0, unroll=UNROLL)

    def lay_south(step):
        under[...] = jnp.where(lat > 0, below[step], 0.0)
        lay(step, under, HALO - 2, HALO - 1)

    def lay_kappas():
        kappas[...] = lax.fori_loop(
            0,
            levels,
            lambda l, k: jnp.where((lane >= l * SLOT) & (lane < (l + 1) * SLOT), coefficients[l], k),
            jnp.zeros((height, LANES), F32),
            unroll=UNROLL,
        )

    def make_faces(step):
        mine, theirs = cols[step], west[step]
        def at(x, p):
            return roll(x, (LANES - p) % LANES) if p else x

        for ref, back in ((face_t, 0), (face_s, 4)):
            speed = at(theirs, 8 - back) + at(mine, 9 - back)
            opened = at(theirs, 10 - back) * at(mine, 11 - back)
            ref[...] = flux(at(theirs, 1), at(mine, 2), theirs, at(mine, 3), speed, opened, kappas[...])

    def advance_yz(step, t_out, s_out, shift):
        tall = height + 8

        def rise(k):
            return pl.ds(HALO - 1 + k, tall)

        def level(l, carry):
            diffuse = coefficients[l]
            down, up = jnp.maximum(l - 1, 0), jnp.minimum(l + 1, levels - 1)
            k_down = jnp.where(l > 0, coefficients[levels + down], 0.0)
            k_up = jnp.where(l < levels - 1, coefficients[levels + jnp.minimum(l, levels - 2)], 0.0)
            o = o_ext[l, own]
            speed_y = v_ext[l, rise(0)] + v_ext[l, rise(1)]
            open_y = o_ext[l, rise(0)] * o_ext[l, rise(1)]
            lift = k_up * (o * o_ext[up, own])
            drop = k_down * (o * o_ext[down, own])
            for ext, out in ((t_ext, t_out), (s_ext, s_out)):
                c = ext[step, l, own]
                flux_y = flux(
                    ext[step, l, rise(0)], ext[step, l, rise(1)], ext[step, l, rise(-1)], ext[step, l, rise(2)],
                    speed_y, open_y, diffuse,
                )
                flux_n = roll(flux_y, tall - 1, 0)
                gain = lift * (ext[step, up, own] - c) - drop * (c - ext[step, down, own])
                out[l, pl.ds(shift, height)] = c + o * (gain - (flux_n[:height] - flux_y[:height]))
            return carry

        lax.fori_loop(0, levels, level, 0, unroll=UNROLL)

    def advance_x(step, t_out, s_out, shift):
        theirs, other = west[step], east[step]
        faces = (face_t[...], face_s[...])

        def level(l, carry):
            base = l * SLOT
            diffuse = coefficients[l]
            u, o = u_own[l], o_ext[l, own]
            u_next = jnp.where(lane == LANES - 1, roll(other, 118 - base), roll(u, LANES - 1))
            o_next = jnp.where(lane == LANES - 1, roll(other, 116 - base), roll(o, LANES - 1))
            speed_x, open_x = u + u_next, o * o_next
            for ext, out, face, back in ((t_ext, t_out, faces[0], 0), (s_ext, s_out, faces[1], 4)):
                c = ext[step, l, own]
                before = jnp.where(lane == 0, roll(theirs, 127 - back - base), roll(c, 1))
                next1 = jnp.where(lane == LANES - 1, roll(other, 125 - back - base), roll(c, LANES - 1))
                next2 = jnp.where(lane >= LANES - 2, roll(other, 124 - back - base), roll(c, LANES - 2))
                flux_x = flux(c, next1, before, next2, speed_x, open_x, diffuse)
                flux_w = jnp.where(lane == 0, roll(face, lax.rem(2 * LANES - back - base, LANES)), roll(flux_x, 1))
                here = pl.ds(shift, height)
                out[l, here] = out[l, here] - o * (flux_x - flux_w)
            return carry

        lax.fori_loop(0, levels, level, 0, unroll=UNROLL)

    def wait_hop(step, tracer, near):
        for k in peers(near):
            hop(step, tracer, near, k).wait_recv()

    def picked(step, tracer, near):
        slots, at = (hop_near, near_slots) if near else (hop_far, far_slots)
        return slots[step][tracer][at[0]], slots[step][tracer][at[1]]

    def second_hop(step):
        for tracer, near in ((1, False), (0, True)):
            wait_hop(step, tracer, near)
            first, second = picked(step, tracer, near)
            first = jnp.take_along_axis(first, order, axis=1)
            second = jnp.take_along_axis(second, order, axis=1)
            relay[step, tracer] = jnp.where(near_part, first, second)
            for k in peers(not near):
                hop(step, tracer, not near, k).start()
            (hop_far if near else hop_near)[step][tracer][0] = relay[step, tracer]

    def choose(step):
        for tracer, near in ((0, False), (1, True)):
            wait_hop(step, tracer, near)
            first, second = picked(step, tracer, near)
            over[step, tracer] = jnp.where(near_part, first, second)

    for copy in first_rows[:6]:
        copy.wait()
    north[0, 1, pl.ds(2 * levels, levels)] = land_rows[0].astype(F32)

    @pl.when(top)
    def _():
        pl.semaphore_wait(barrier, expected)
        first_hop(0)

    for copy in first_rows[6:]:
        copy.wait()
    south[0, 1, pl.ds(2 * levels, levels)] = land_rows[1].astype(F32)
    for load in loads:
        load.wait()

    def ocean(l, carry):
        o_ext[l, own] = land_own[l].astype(F32)
        return carry

    lax.fori_loop(0, levels, ocean, 0, unroll=UNROLL)
    pack_cols(0)

    @pl.when(jnp.logical_not(top))
    def _():
        pl.semaphore_wait(barrier, expected)

    to_right(0).start()
    to_left(0).start()

    @pl.when(lat < nlat - 1)
    def _():
        to_north(0).start()

    @pl.when(lat > 0)
    def _():
        to_south(0).start()

    lay_kappas()

    @pl.when(top)
    def _():
        crown()

    def send_cols(step):
        pack_cols(step)
        to_right(step).start()
        to_left(step).start()

    shift = (partner[0] + lon * LANES) & (nlon * LANES - 1)
    tile, offset = shift // LANES, shift & (LANES - 1)
    tile_far, tile_place = tile // WIDE, lax.rem(tile, WIDE)
    edge_lane = lax.broadcasted_iota(jnp.int32, (EDGE, LANES), 1)
    order = (offset - edge_lane) & (LANES - 1)
    near_part = edge_lane <= offset
    borrow0 = jnp.where(tile_place < place, 1, 0)
    borrow1 = jnp.where(tile_place - 1 < place, 1, 0)

    near_slots = [lax.rem(2 * place - tile_place + i + WIDE, WIDE) for i in range(2)]
    far_slots = [lax.rem(2 * far - tile_far + borrow + 2 * groups, groups) for borrow in (borrow0, borrow1)]

    for step in range(STEPS):
        last = step == STEPS - 1
        t_out, s_out, at = (temp_out, salt_out, 0) if last else (t_ext.at[step + 1], s_ext.at[step + 1], HALO)
        if step:

            @pl.when(top)
            def _():
                send_cols(step)

        @pl.when(top)
        def _():
            second_hop(step)

        @pl.when(lat > 0)
        def _():
            to_north(step).wait_recv()

        lay_south(step)

        @pl.when(lat < nlat - 1)
        def _():
            to_south(step).wait_recv()
            lay(step, above.at[step], end, end)

        advance_yz(step, t_out, s_out, at)
        to_right(step).wait_recv()
        to_left(step).wait_recv()
        make_faces(step)
        advance_x(step, t_out, s_out, at)
        if not last:

            @pl.when(jnp.logical_not(top))
            def _():
                send_cols(step + 1)

            pack_rows(step + 1, south, HALO)

            @pl.when(lat > 0)
            def _():
                to_south(step + 1).start()

            pack_rows(step + 1, north, end - 2)

            @pl.when(lat < nlat - 1)
            def _():
                to_north(step + 1).start()

        @pl.when(top)
        def _():
            choose(step)
            mend(step)
            if not last:
                both = pl.ds(0, 2 * levels)
                for tracer in range(2):
                    north[step + 1, tracer, both] = north[step + 1, tracer, both] - mending[tracer, both]
                first_hop(step + 1)
            mend_rows(t_out, s_out, at + height - 2)

    for step in range(STEPS):
        to_right(step).wait_send()
        to_left(step).wait_send()

        @pl.when(lat < nlat - 1)
        def _():
            to_north(step).wait_send()

        @pl.when(lat > 0)
        def _():
            to_south(step).wait_send()

        @pl.when(top)
        def _():
            for tracer in range(2):
                for near in (True, False):
                    for k in peers(near):
                        hop(step, tracer, near, k).wait_send()


def hand_over(temp, salt, temp_out, salt_out, sem):
    copies = [pltpu.make_async_copy(a, b, sem.at[i]) for i, (a, b) in enumerate(((temp, temp_out), (salt, salt_out)))]
    for copy in copies:
        copy.start()
    for copy in copies:
        copy.wait()


def local(nlon, nlat, temp, salt, u_vel, v_vel, land_sea, partner, kappa_h, kappa_v):
    levels, height, width = temp.shape
    block = jax.ShapeDtypeStruct(temp.shape, F32)
    anywhere = pl.BlockSpec(memory_space=pl.ANY)
    groups = nlon // WIDE

    def room(*shape):
        return pltpu.VMEM(shape, F32)

    tall = height + 24
    results = pl.pallas_call(
        functools.partial(kernel, nlon, nlat),
        out_shape=(block, block),
        in_specs=[anywhere] * 7,
        out_specs=[pl.BlockSpec(memory_space=pltpu.VMEM)] * 2,
        scratch_shapes=[
            pltpu.SMEM(partner.shape, jnp.int32),
            pltpu.SMEM((2 * levels - 1,), F32),
            room(STEPS, levels, tall, width),
            room(STEPS, levels, tall, width),
            room(levels, tall, width),
            room(levels, tall, width),
            room(levels, height, width),
            pltpu.VMEM((levels, height, width), jnp.int32),
            pltpu.VMEM((2, levels, width), jnp.int32),
            room(STEPS, height, width),
            room(STEPS, 2, EDGE, width),
            room(STEPS, 2, EDGE, width),
            room(STEPS, 2, EDGE, width),
            room(STEPS, height, width),
            room(STEPS, height, width),
            room(STEPS, 2, EDGE, width),
            room(STEPS, 2, EDGE, width),
            *[room(WIDE, EDGE, width)] * (2 * STEPS),
            *[room(groups, EDGE, width)] * (2 * STEPS),
            room(2, EDGE, width),
            room(STEPS, 2, EDGE, width),
            room(3, 16, width),
            room(2, EDGE, width),
            room(height, width),
            room(height, width),
            room(height, width),
            pltpu.SemaphoreType.DMA((7,)),
            pltpu.SemaphoreType.DMA((12,)),
            pltpu.SemaphoreType.DMA((STEPS, 4)),
            pltpu.SemaphoreType.DMA((STEPS, 4)),
            pltpu.SemaphoreType.DMA((STEPS, 2, WIDE)),
            pltpu.SemaphoreType.DMA((STEPS, 2, WIDE)),
            pltpu.SemaphoreType.DMA((STEPS, 2, groups)),
            pltpu.SemaphoreType.DMA((STEPS, 2, groups)),
        ],
        compiler_params=pltpu.CompilerParams(collective_id=0, has_side_effects=True, vmem_limit_bytes=54880 << 10),
        name="tracer_steps",
    )(temp, salt, u_vel, v_vel, land_sea, partner, jnp.concatenate([kappa_h, kappa_v]))
    return results


def solution(mesh):
    field = P(None, "lat", "lon")
    return jax.shard_map(
        functools.partial(local, mesh.shape["lon"], mesh.shape["lat"]),
        mesh=mesh,
        in_specs=(field,) * 5 + (P("lon"), P(), P()),
        out_specs=(field, field),
        check_vma=False,
    )
```

```python
import functools

import jax
import jax.numpy as jnp
from jax import lax
from jax.experimental import pallas as pl
from jax.experimental.pallas import tpu as pltpu
from jax.sharding import PartitionSpec as P

STEPS = 2
WIDE = 8
LANES = 128
SLOT = 12
EDGE = 32
UNROLL = 5
F32 = jnp.float32
MESH = pl.DeviceIdType.MESH
HALO = 8


def roll(x, shift, axis=1):
    return pltpu.roll(x, shift, axis)


def flux(c0, c1, before, after, speed, opened, diffuse):
    return opened * (speed * ((7.0 * (c0 + c1) - (before + after)) * (1.0 / 24.0)) - diffuse * (c1 - c0))


def kernel(
    nlon, nlat, temp, salt, u_vel, v_vel, land, partner_in, kappas_in, temp_out, salt_out, unit,
    partner, coefficients,
    t_ext, s_ext, v_ext, o_ext, u_own, land_own, land_rows, cols, north, south, relay, west, east, below, above,
    near00, near01, near10, near11, far00, far01, far10, far11, under, over, under_top, mending,
    face_t, face_s, kappas,
    load_sem, row_sem, send, recv, near_send, near_recv, far_send, far_recv,
):
    hop_near, hop_far = ((near00, near01), (near10, near11)), ((far00, far01), (far10, far11))
    levels, height, _ = temp.shape
    end = HALO + height
    lon, lat = lax.axis_index("lon"), lax.axis_index("lat")
    top = lat == nlat - 1
    right, left = lax.rem(lon + 1, nlon), lax.rem(lon + nlon - 1, nlon)
    place, far = lax.rem(lon, WIDE), lon // WIDE
    groups = nlon // WIDE

    def farthest_first(count):
        return sorted(range(1, count), key=lambda k: -min(k, count - k))

    def in_group(k):
        return far * WIDE + lax.rem(place + k, WIDE)

    def in_across(k):
        return lax.rem(far + k, groups) * WIDE + place

    def row_copy(field, row, dst, i):
        return pltpu.make_async_copy(field.at[:, row], dst, row_sem.at[i])

    first_rows = [
        row_copy(temp, height - 2, north.at[0, 0, pl.ds(0, levels)], 0),
        row_copy(temp, height - 1, north.at[0, 0, pl.ds(levels, levels)], 1),
        row_copy(v_vel, height - 1, north.at[0, 0, pl.ds(2 * levels, levels)], 2),
        row_copy(salt, height - 2, north.at[0, 1, pl.ds(0, levels)], 3),
        row_copy(salt, height - 1, north.at[0, 1, pl.ds(levels, levels)], 4),
        row_copy(land, height - 1, land_rows.at[0], 5),
        row_copy(temp, 0, south.at[0, 0, pl.ds(0, levels)], 6),
        row_copy(temp, 1, south.at[0, 0, pl.ds(levels, levels)], 7),
        row_copy(v_vel, 0, south.at[0, 0, pl.ds(2 * levels, levels)], 8),
        row_copy(salt, 0, south.at[0, 1, pl.ds(0, levels)], 9),
        row_copy(salt, 1, south.at[0, 1, pl.ds(levels, levels)], 10),
        row_copy(land, 0, land_rows.at[1], 11),
    ]
    loads = [
        pltpu.make_async_copy(src, dst, load_sem.at[i])
        for i, (src, dst) in enumerate(
            (
                (temp, t_ext.at[0, :, pl.ds(HALO, height)]),
                (salt, s_ext.at[0, :, pl.ds(HALO, height)]),
                (v_vel, v_ext.at[:, pl.ds(HALO, height)]),
                (land, land_own),
                (u_vel, u_own),
                (partner_in, partner),
                (kappas_in, coefficients),
            )
        )
    ]
    barrier = pltpu.get_barrier_semaphore()

    def greet(a, b):
        pl.semaphore_signal(barrier, inc=1, device_id=(a, b), device_id_type=MESH)

    @pl.when(top)
    def _():
        for k in farthest_first(groups):
            greet(in_across(k), lat)
        for k in farthest_first(WIDE):
            greet(in_group(k), lat)

    greet(right, lat)
    greet(left, lat)

    @pl.when(lat > 0)
    def _():
        greet(lon, lat - 1)

    @pl.when(lat < nlat - 1)
    def _():
        greet(lon, lat + 1)

    expected = 2 + jnp.where(lat > 0, 1, 0) + jnp.where(top, WIDE + groups - 2, 1)

    for copy in first_rows + loads:
        copy.start()

    def remote(src, dst, sent, got, a, b):
        return pltpu.make_async_remote_copy(
            src_ref=src, dst_ref=dst, send_sem=sent, recv_sem=got, device_id=(a, b), device_id_type=MESH
        )

    def rows(step):
        return pl.ds(0, (3 if step == 0 else 2) * levels)

    def to_right(step):
        return remote(cols.at[step], west.at[step], send.at[step, 0], recv.at[step, 0], right, lat)

    def to_left(step):
        return remote(cols.at[step], east.at[step], send.at[step, 1], recv.at[step, 1], left, lat)

    def to_north(step):
        return remote(
            north.at[step, :, rows(step)], below.at[step, :, rows(step)], send.at[step, 2], recv.at[step, 2],
            lon, lax.rem(lat + 1, nlat),
        )

    def to_south(step):
        return remote(
            south.at[step, :, rows(step)], above.at[step, :, rows(step)], send.at[step, 3], recv.at[step, 3],
            lon, lax.rem(lat + nlat - 1, nlat),
        )

    def hop(step, tracer, near, k):
        message = (north if near == (tracer == 0) else relay).at[step, tracer, rows(step)]
        slots, sent, got, to = (
            (hop_near, near_send, near_recv, in_group) if near else (hop_far, far_send, far_recv, in_across)
        )
        return remote(
            message, slots[step][tracer].at[k, rows(step)], sent.at[step, tracer, k], got.at[step, tracer, k], to(k), lat
        )

    def peers(near):
        return farthest_first(WIDE if near else groups)

    def first_hop(step):
        for k in range(max(WIDE, groups)):
            for tracer, near in ((0, True), (1, False)):
                if k < len(peers(near)):
                    hop(step, tracer, near, peers(near)[k]).start()
        hop_near[step][0][0] = north[step, 0]
        hop_far[step][1][0] = north[step, 1]

    def pack_rows(step, ref, row):
        def level(l, carry):
            for tracer, ext in enumerate((t_ext, s_ext)):
                for i in range(2):
                    ref[step, tracer, pl.ds(i * levels + l, 1)] = ext[step, l, pl.ds(row + i, 1)]
            return carry

        lax.fori_loop(0, levels, level, 0, unroll=UNROLL)

    lane = lax.broadcasted_iota(jnp.int32, (height, LANES), 1)
    own = pl.ds(HALO, height)

    def pack_cols(step):
        def level(l, held):
            base = l * SLOT
            here = lane - base
            held = jnp.where((here >= 0) & (here < 4), roll(t_ext[step, l, own], base + 2), held)
            held = jnp.where((here >= 4) & (here < 8), roll(s_ext[step, l, own], base + 6), held)
            if step == 0:
                held = jnp.where((here >= 8) & (here < 10), roll(u_own[l], base + 9), held)
                held = jnp.where((here >= 10) & (here < 12), roll(o_ext[l, own], base + 11), held)
            return held

        cols[step] = lax.fori_loop(0, levels, level, cols[0] if step else jnp.zeros((height, LANES), F32), unroll=UNROLL)

    def lay(step, source, row, still):
        def level(l, carry):
            for tracer, ext in enumerate((t_ext, s_ext)):
                for i in range(2):
                    ext[step, l, pl.ds(row + i, 1)] = source[tracer, pl.ds(i * levels + l, 1)]
            if step == 0:
                v_ext[l, pl.ds(still, 1)] = source[0, pl.ds(2 * levels + l, 1)]
                o_ext[l, pl.ds(still, 1)] = source[1, pl.ds(2 * levels + l, 1)]
            return carry

        lax.fori_loop(0, levels, level, 0, unroll=UNROLL)

    def crown():
        above_own = jnp.zeros((2, LANES), F32)

        def level(l, carry):
            for step in range(STEPS):
                t_ext[step, l, pl.ds(end, 2)] = above_own
                s_ext[step, l, pl.ds(end, 2)] = above_own
            v_ext[l, pl.ds(end, 2)] = above_own
            o_ext[l, pl.ds(end, 2)] = above_own
            under_top[0, pl.ds(l, 1)] = v_ext[l, pl.ds(end - 2, 1)]
            under_top[1, pl.ds(l, 1)] = o_ext[l, pl.ds(end - 2, 1)]
            under_top[2, pl.ds(l, 1)] = jnp.full((1, LANES), coefficients[l], F32)
            return carry

        lax.fori_loop(0, levels, level, 0, unroll=UNROLL)

    def mend(step):
        first, second, still = pl.ds(0, levels), pl.ds(levels, levels), pl.ds(2 * levels, levels)
        every = pl.ds(0, levels)
        v2, o2, diffuse = under_top[0, every], under_top[1, every], under_top[2, every]
        v1, o1 = north[0, 0, still], north[0, 1, still]
        v_ghost, o_ghost = -over[0, 0, still], over[0, 1, still]
        lower = o2 * o1 * (v2 + v1) * (-1.0 / 24.0)
        speed, opened = v1 + v_ghost, o1 * o_ghost
        for tracer in range(2):
            c2, c1 = north[step, tracer, first], north[step, tracer, second]
            g1, g2 = over[step, tracer, second], over[step, tracer, first]
            missing = lower * g1
            face = flux(c1, g1, c2, g2, speed, opened, diffuse)
            mending[tracer, first] = o2 * missing
            mending[tracer, second] = o1 * (face - missing)

    def mend_rows(t_out, s_out, row):
        def level(l, carry):
            for tracer, out in enumerate((t_out, s_out)):
                for i in range(2):
                    here = pl.ds(row + i, 1)
                    out[l, here] = out[l, here] - mending[tracer, pl.ds(i * levels + l, 1)]
            return carry

        lax.fori_loop(0, levels, level, 0, unroll=UNROLL)

    def lay_south(step):
        under[...] = jnp.where(lat > 0, below[step], 0.0)
        lay(step, under, HALO - 2, HALO - 1)

    def lay_kappas():
        kappas[...] = lax.fori_loop(
            0,
            levels,
            lambda l, k: jnp.where((lane >= l * SLOT) & (lane < (l + 1) * SLOT), coefficients[l], k),
            jnp.zeros((height, LANES), F32),
            unroll=UNROLL,
        )

    def make_faces(step):
        mine, theirs = cols[step], west[step]
        def at(x, p):
            return roll(x, (LANES - p) % LANES) if p else x

        for ref, back in ((face_t, 0), (face_s, 4)):
            speed = at(theirs, 8 - back) + at(mine, 9 - back)
            opened = at(theirs, 10 - back) * at(mine, 11 - back)
            ref[...] = flux(at(theirs, 1), at(mine, 2), theirs, at(mine, 3), speed, opened, kappas[...])

    def advance_yz(step, t_out, s_out, shift):
        tall = height + 8

        def rise(k):
            return pl.ds(HALO - 1 + k, tall)

        def level(l, carry):
            diffuse = coefficients[l]
            down, up = jnp.maximum(l - 1, 0), jnp.minimum(l + 1, levels - 1)
            k_down = jnp.where(l > 0, coefficients[levels + down], 0.0)
            k_up = jnp.where(l < levels - 1, coefficients[levels + jnp.minimum(l, levels - 2)], 0.0)
            o = o_ext[l, own]
            speed_y = v_ext[l, rise(0)] + v_ext[l, rise(1)]
            open_y = o_ext[l, rise(0)] * o_ext[l, rise(1)]
            lift = k_up * (o * o_ext[up, own])
            drop = k_down * (o * o_ext[down, own])
            for ext, out in ((t_ext, t_out), (s_ext, s_out)):
                c = ext[step, l, own]
                flux_y = flux(
                    ext[step, l, rise(0)], ext[step, l, rise(1)], ext[step, l, rise(-1)], ext[step, l, rise(2)],
                    speed_y, open_y, diffuse,
                )
                flux_n = roll(flux_y, tall - 1, 0)
                gain = lift * (ext[step, up, own] - c) - drop * (c - ext[step, down, own])
                out[l, pl.ds(shift, height)] = c + o * (gain - (flux_n[:height] - flux_y[:height]))
            return carry

        lax.fori_loop(0, levels, level, 0, unroll=UNROLL)

    def advance_x(step, t_out, s_out, shift):
        theirs, other = west[step], east[step]
        faces = (face_t[...], face_s[...])

        def level(l, carry):
            base = l * SLOT
            diffuse = coefficients[l]
            u, o = u_own[l], o_ext[l, own]
            u_next = jnp.where(lane == LANES - 1, roll(other, 118 - base), roll(u, LANES - 1))
            o_next = jnp.where(lane == LANES - 1, roll(other, 116 - base), roll(o, LANES - 1))
            speed_x, open_x = u + u_next, o * o_next
            for ext, out, face, back in ((t_ext, t_out, faces[0], 0), (s_ext, s_out, faces[1], 4)):
                c = ext[step, l, own]
                before = jnp.where(lane == 0, roll(theirs, 127 - back - base), roll(c, 1))
                next1 = jnp.where(lane == LANES - 1, roll(other, 125 - back - base), roll(c, LANES - 1))
                next2 = jnp.where(lane >= LANES - 2, roll(other, 124 - back - base), roll(c, LANES - 2))
                flux_x = flux(c, next1, before, next2, speed_x, open_x, diffuse)
                flux_w = jnp.where(lane == 0, roll(face, lax.rem(2 * LANES - back - base, LANES)), roll(flux_x, 1))
                here = pl.ds(shift, height)
                out[l, here] = out[l, here] - o * (flux_x - flux_w)
            return carry

        lax.fori_loop(0, levels, level, 0, unroll=UNROLL)

    def wait_hop(step, tracer, near):
        for k in peers(near):
            hop(step, tracer, near, k).wait_recv()

    def picked(step, tracer, near):
        slots, at = (hop_near, near_slots) if near else (hop_far, far_slots)
        return slots[step][tracer][at[0]], slots[step][tracer][at[1]]

    def second_hop(step):
        for tracer, near in ((1, False), (0, True)):
            wait_hop(step, tracer, near)
            first, second = picked(step, tracer, near)
            first = jnp.take_along_axis(first, order, axis=1)
            second = jnp.take_along_axis(second, order, axis=1)
            relay[step, tracer] = jnp.where(near_part, first, second)
            for k in peers(not near):
                hop(step, tracer, not near, k).start()
            (hop_far if near else hop_near)[step][tracer][0] = relay[step, tracer]

    def choose(step):
        for tracer, near in ((0, False), (1, True)):
            wait_hop(step, tracer, near)
            first, second = picked(step, tracer, near)
            over[step, tracer] = jnp.where(near_part, first, second)

    for copy in first_rows[:6]:
        copy.wait()
    north[0, 1, pl.ds(2 * levels, levels)] = land_rows[0].astype(F32)

    @pl.when(top)
    def _():
        pl.semaphore_wait(barrier, expected)
        first_hop(0)

    for copy in first_rows[6:]:
        copy.wait()
    south[0, 1, pl.ds(2 * levels, levels)] = land_rows[1].astype(F32)
    for load in loads:
        load.wait()

    def ocean(l, carry):
        o_ext[l, own] = land_own[l].astype(F32)
        return carry

    lax.fori_loop(0, levels, ocean, 0, unroll=UNROLL)
    pack_cols(0)

    @pl.when(jnp.logical_not(top))
    def _():
        pl.semaphore_wait(barrier, expected)

    to_right(0).start()
    to_left(0).start()

    @pl.when(lat < nlat - 1)
    def _():
        to_north(0).start()

    @pl.when(lat > 0)
    def _():
        to_south(0).start()

    lay_kappas()
    unit[...] = jnp.ones_like(unit)

    @pl.when(top)
    def _():
        crown()

    def send_cols(step):
        pack_cols(step)
        to_right(step).start()
        to_left(step).start()

    shift = (partner[0] + lon * LANES) & (nlon * LANES - 1)
    tile, offset = shift // LANES, shift & (LANES - 1)
    tile_far, tile_place = tile // WIDE, lax.rem(tile, WIDE)
    edge_lane = lax.broadcasted_iota(jnp.int32, (EDGE, LANES), 1)
    order = (offset - edge_lane) & (LANES - 1)
    near_part = edge_lane <= offset
    borrow0 = jnp.where(tile_place < place, 1, 0)
    borrow1 = jnp.where(tile_place - 1 < place, 1, 0)

    near_slots = [lax.rem(2 * place - tile_place + i + WIDE, WIDE) for i in range(2)]
    far_slots = [lax.rem(2 * far - tile_far + borrow + 2 * groups, groups) for borrow in (borrow0, borrow1)]

    for step in range(STEPS):
        last = step == STEPS - 1
        t_out, s_out, at = (temp_out, salt_out, 0) if last else (t_ext.at[step + 1], s_ext.at[step + 1], HALO)
        if step:

            @pl.when(top)
            def _():
                send_cols(step)

        @pl.when(top)
        def _():
            second_hop(step)

        @pl.when(lat > 0)
        def _():
            to_north(step).wait_recv()

        lay_south(step)

        @pl.when(lat < nlat - 1)
        def _():
            to_south(step).wait_recv()
            lay(step, above.at[step], end, end)

        advance_yz(step, t_out, s_out, at)
        to_right(step).wait_recv()
        to_left(step).wait_recv()
        make_faces(step)
        advance_x(step, t_out, s_out, at)
        if not last:

            @pl.when(jnp.logical_not(top))
            def _():
                send_cols(step + 1)

            pack_rows(step + 1, south, HALO)

            @pl.when(lat > 0)
            def _():
                to_south(step + 1).start()

            pack_rows(step + 1, north, end - 2)

            @pl.when(lat < nlat - 1)
            def _():
                to_north(step + 1).start()

        @pl.when(top)
        def _():
            choose(step)
            mend(step)
            if not last:
                both = pl.ds(0, 2 * levels)
                for tracer in range(2):
                    north[step + 1, tracer, both] = north[step + 1, tracer, both] - mending[tracer, both]
                first_hop(step + 1)
            mend_rows(t_out, s_out, at + height - 2)

    for step in range(STEPS):
        to_right(step).wait_send()
        to_left(step).wait_send()

        @pl.when(lat < nlat - 1)
        def _():
            to_north(step).wait_send()

        @pl.when(lat > 0)
        def _():
            to_south(step).wait_send()

        @pl.when(top)
        def _():
            for tracer in range(2):
                for near in (True, False):
                    for k in peers(near):
                        hop(step, tracer, near, k).wait_send()


def hand_over(temp, salt, temp_out, salt_out, sem):
    copies = [pltpu.make_async_copy(a, b, sem.at[i]) for i, (a, b) in enumerate(((temp, temp_out), (salt, salt_out)))]
    for copy in copies:
        copy.start()
    for copy in copies:
        copy.wait()


def local(nlon, nlat, temp, salt, u_vel, v_vel, land_sea, partner, kappa_h, kappa_v):
    levels, height, width = temp.shape
    block = jax.ShapeDtypeStruct(temp.shape, F32)
    anywhere = pl.BlockSpec(memory_space=pl.ANY)
    groups = nlon // WIDE

    def room(*shape):
        return pltpu.VMEM(shape, F32)

    tall = height + 24
    new_temp, new_salt, unit = pl.pallas_call(
        functools.partial(kernel, nlon, nlat),
        out_shape=(block, block, jax.ShapeDtypeStruct((width,), F32)),
        in_specs=[anywhere] * 7,
        out_specs=[pl.BlockSpec(memory_space=pltpu.VMEM)] * 3,
        scratch_shapes=[
            pltpu.SMEM(partner.shape, jnp.int32),
            pltpu.SMEM((2 * levels - 1,), F32),
            room(STEPS, levels, tall, width),
            room(STEPS, levels, tall, width),
            room(levels, tall, width),
            room(levels, tall, width),
            room(levels, height, width),
            pltpu.VMEM((levels, height, width), jnp.int32),
            pltpu.VMEM((2, levels, width), jnp.int32),
            room(STEPS, height, width),
            room(STEPS, 2, EDGE, width),
            room(STEPS, 2, EDGE, width),
            room(STEPS, 2, EDGE, width),
            room(STEPS, height, width),
            room(STEPS, height, width),
            room(STEPS, 2, EDGE, width),
            room(STEPS, 2, EDGE, width),
            *[room(WIDE, EDGE, width)] * (2 * STEPS),
            *[room(groups, EDGE, width)] * (2 * STEPS),
            room(2, EDGE, width),
            room(STEPS, 2, EDGE, width),
            room(3, 16, width),
            room(2, EDGE, width),
            room(height, width),
            room(height, width),
            room(height, width),
            pltpu.SemaphoreType.DMA((7,)),
            pltpu.SemaphoreType.DMA((12,)),
            pltpu.SemaphoreType.DMA((STEPS, 4)),
            pltpu.SemaphoreType.DMA((STEPS, 4)),
            pltpu.SemaphoreType.DMA((STEPS, 2, WIDE)),
            pltpu.SemaphoreType.DMA((STEPS, 2, WIDE)),
            pltpu.SemaphoreType.DMA((STEPS, 2, groups)),
            pltpu.SemaphoreType.DMA((STEPS, 2, groups)),
        ],
        compiler_params=pltpu.CompilerParams(collective_id=0, has_side_effects=True, vmem_limit_bytes=54880 << 10),
        name="tracer_steps",
    )(temp, salt, u_vel, v_vel, land_sea, partner, jnp.concatenate([kappa_h, kappa_v]))
    return new_temp * unit, new_salt * unit


def solution(mesh):
    field = P(None, "lat", "lon")
    return jax.shard_map(
        functools.partial(local, mesh.shape["lon"], mesh.shape["lat"]),
        mesh=mesh,
        in_specs=(field,) * 5 + (P("lon"), P(), P()),
        out_specs=(field, field),
        check_vma=False,
    )
```
